256 devices in a mesh: shard: 4 (over y_lo, core), replica: 64 (over z, y_hi, x).
Axes of the slice: x: 4, y: 4 (y_hi: 2, y_lo: 2; y = y_hi * 2 + y_lo), z: 8, core: 2. Of those that a mesh axis runs over, the one named last changes fastest.
Arguments:
- tokens_in: bfloat16 [65536, 8192], P(('shard', 'replica')), may hold values from -6 to 6
- key_cotangent: bfloat16 [65536, 512], P(('shard', 'replica')), may hold values from -6 to 6
- key_weight: bfloat16 [8192, 512], P('shard'), may hold values from -0.0625 to 0.0625
- master_store: float32 [8192, 512], P(('shard', 'replica')), may hold values from -0.015625 to 0.015625
- first_moment: float32 [8192, 512], P(('shard', 'replica')), may hold values from -4 to 4
- second_moment: float32 [8192, 512], P(('shard', 'replica')), may hold values from 0.25 to 4
- writer: int32 [4, 64], P('shard'), may hold values from 0 to 63, each once within a row
Outputs:
- input_grad: bfloat16 [65536, 8192], P(('shard', 'replica'))
- master_new: float32 [8192, 512], P(('shard', 'replica'))
- moment_one: float32 [8192, 512], P(('shard', 'replica'))
- moment_two: float32 [8192, 512], P(('shard', 'replica'))
- weight_new: bfloat16 [8192, 512], P('shard')
The draws below stay inside these ranges and needn't reach their ends.
Inputs may be any that keep to these rules, and one draw needn't show every extreme that they name: Each row is a permutation: replica r of shard s holds the states of row block writer[s, r] of that shard.
All inputs are finite; a program needn't handle non-finite values.
Results may differ from the reference program's by a relative error of at most 0.0027.
Values may be sent and summed in bfloat16 or wider, within the bound.
No kernel may reach another device: no remote copies, remote signals or barrier semaphores. Data moves between devices by JAX's collectives and lax.ppermute only.
A program may use at most 128 MiB of HBM per device.

```python
import math
import jax
import jax.numpy as jnp
from jax import lax

D = 8192
TOK_DEV = 256
KW = 512
TOKENS = 65536
BR = 32
N_SHARD = 4
N_REPLICA = 64


def steps_of(stream_key, extent, shards, least, largest):
    loudness, own = 1.0, jax.random.fold_in(stream_key, 6)
    for position, parts in shards:
        draws = jnp.exp(jax.random.uniform(jax.random.fold_in(own, position), (parts,), jnp.float32, least / len(shards), largest / len(shards)))
        loudness = loudness * jnp.repeat(draws, extent[position] // parts).reshape([-1 if axis == position else 1 for axis in range(len(extent))])
    return loudness


def gaussian(stream_key, shape, width, limit, split=(), kind=jnp.bfloat16):
    result = jax.random.normal(stream_key, shape, jnp.float32) * width
    if len(split) > 0:
        result = steps_of(stream_key, shape, split, -0.22, 0.18) * result
    return jnp.clip(result, min=-limit, max=limit).astype(kind)


def setup_inputs(seed: int = 0) -> dict:
    arg_keys = jax.random.split(jax.random.key(seed), 8)
    return {
        "tokens_in": gaussian(arg_keys[0], (TOKENS, D), 1.0, 6.0, ((0, 256),)),
        "key_cotangent": gaussian(arg_keys[1], (TOKENS, KW), 1.0, 6.0, ((0, 256),)),
        "key_weight": gaussian(arg_keys[2], (D, KW), D ** -0.5, 0.0625, ((0, 4),)),
        "master_store": gaussian(arg_keys[3], (D, KW), 0.001, 0.015625, ((0, 256),), jnp.float32),
        "first_moment": gaussian(arg_keys[4], (D, KW), 0.5, 4.0, ((0, 256),), jnp.float32),
        "second_moment": jnp.clip(jnp.exp(math.log(4.0) - 2.7725887 * jax.random.uniform(arg_keys[5], (D, KW), jnp.float32) ** steps_of(arg_keys[5], (D, KW), ((0, 256),), -0.2, 0.2)), 0.25, 4.0),
        "writer": jax.vmap(lambda own: jax.random.permutation(own, N_REPLICA))(jax.random.split(arg_keys[6], N_SHARD)).reshape((N_SHARD, N_REPLICA)).astype(jnp.int32),
    }


beta_first = 0.9
beta_second = 0.95
learn_rate = 0.0003
decay_rate = 0.1
adam_eps = 1e-08
step_count = 100

def reference(tokens_in, key_cotangent, key_weight, master_store, first_moment, second_moment, writer):
    input_grad = jnp.dot(key_cotangent, key_weight.T, preferred_element_type=jnp.float32).astype(jnp.bfloat16)
    groups_x = tokens_in.reshape(N_SHARD * N_REPLICA, TOK_DEV, D)
    groups_k = key_cotangent.reshape(N_SHARD * N_REPLICA, TOK_DEV, KW)

    def accumulate(carry, pair):
        partial_value = jnp.dot(pair[0].T, pair[1], preferred_element_type=jnp.float32).astype(jnp.bfloat16)
        return (carry + partial_value.astype(jnp.float32), None)
    summed, _ = lax.scan(accumulate, jnp.zeros((D, KW), jnp.float32), (groups_x, groups_k))
    weight_grad = summed * TOKENS ** (-0.5)
    blocks = weight_grad.reshape(N_SHARD, N_REPLICA, BR, KW)
    stored_grad = jnp.take_along_axis(blocks, writer[:, :, None, None].astype(jnp.int32), axis=1).reshape(D, KW)
    moment_one = beta_first * first_moment + (1.0 - beta_first) * stored_grad
    moment_two = beta_second * second_moment + (1.0 - beta_second) * stored_grad * stored_grad
    corrected_one = moment_one / (1.0 - beta_first ** step_count)
    corrected_two = moment_two / (1.0 - beta_second ** step_count)
    master_new = master_store - learn_rate * (corrected_one / (jnp.sqrt(corrected_two) + adam_eps) + decay_rate * master_store)
    stored = master_new.reshape(N_SHARD, N_REPLICA, BR, KW)
    shard_ids = jnp.arange(N_SHARD, dtype=jnp.int32)[:, None]
    placed = jnp.zeros_like(stored).at[shard_ids, writer.astype(jnp.int32)].set(stored)
    weight_new = placed.reshape(D, KW).astype(jnp.bfloat16)
    return (input_grad, master_new, moment_one, moment_two, weight_new)
```

```python
import functools

import jax
import jax.numpy as jnp
from jax import lax
from jax.experimental import pallas as pl
from jax.experimental.pallas import tpu as pltpu
from jax.sharding import Mesh
from jax.sharding import PartitionSpec as P

beta_first = 0.9
beta_second = 0.95
learn_rate = 0.0003
decay_rate = 0.1
adam_eps = 1e-08
step_count = 100

NYL, NC, NZ, NYH, NX = 2, 2, 8, 2, 4
NY = NYL * NYH
AXES = ("yl", "c", "z", "yh", "x")
VMEM_LIMIT = 48 * 1024 * 1024


def shift(axis, step):
    if axis == "y":
        spot = lambda y: (y % NYL) * NYH + y // NYL
        return [(spot(y), spot((y + step) % NY)) for y in range(NY)]
    size = {"x": NX, "z": NZ, "c": NC, "yl": NYL, "yh": NYH}[axis]
    return [(i, (i + step) % size) for i in range(size)]


def send(value, axis, step):
    return lax.ppermute(value, ("yl", "yh") if axis == "y" else axis, shift(axis, step))


def vmem():
    return pl.BlockSpec(memory_space=pltpu.VMEM)


def both_cores_kernel(far, place, order, own_tok, own_key, got_tok, got_key, *rest):
    outs, total = rest[:-1], rest[-1]
    x, y, z = place[0], place[1], place[2]
    rows, half = total.shape[0], outs[0].shape[2]
    cut = min(512, rows)
    for q in range(rows // cut):
        piece = slice(q * cut, (q + 1) * cut)

        def partial(tok, key):
            value = lax.dot_general(
                tok[:, piece], key[...], (((0,), (0,)), ((), ())), preferred_element_type=jnp.float32
            )
            return value.astype(jnp.bfloat16).astype(jnp.float32)

        total[piece, :] = partial(own_tok, own_key) + partial(got_tok, got_key)
    steps_y = (1, 3) if far else (0, 2)
    for k in range(NX):
        to_x = lax.rem(x + k, NX)
        for n, j in enumerate(steps_y):
            to_yh = lax.div(lax.rem(y + j, NY), NYL)
            for m in range(NZ):
                to_z = lax.rem(z + m, NZ)
                block = order[0, (to_z * NYH + to_yh) * NX + to_x]
                start = pl.multiple_of(block * (2 * half), 2 * half)
                first = total[pl.ds(start, half), :]
                second = total[pl.ds(start + half, half), :]
                outs[k][n, m] = first.astype(outs[k].dtype)
                outs[NX + n][k, m] = second.astype(outs[NX + n].dtype)


def both_cores(far, place, order, own_tok, own_key, got_tok, got_key, block_rows):
    rows, width = got_tok.shape[1], own_key.shape[1]
    half = block_rows // 2
    near = jnp.bfloat16 if far else jnp.float32
    shapes = [
        jax.ShapeDtypeStruct((2, NZ, half, width), jnp.float32 if k == 0 else jnp.bfloat16)
        for k in range(NX)
    ]
    shapes += [
        jax.ShapeDtypeStruct((NX, NZ, half, width), near if n == 0 else jnp.bfloat16)
        for n in range(2)
    ]
    return pl.pallas_call(
        functools.partial(both_cores_kernel, far),
        grid_spec=pltpu.PrefetchScalarGridSpec(
            num_scalar_prefetch=2,
            grid=(1,),
            in_specs=[
                pl.BlockSpec((own_tok.shape[0], rows), lambda i, place, order: (0, place[3])),
                vmem(),
                vmem(),
                vmem(),
            ],
            out_specs=[vmem()] * len(shapes),
            scratch_shapes=[pltpu.VMEM((rows, width), jnp.float32)],
        ),
        out_shape=shapes,
        compiler_params=pltpu.CompilerParams(vmem_limit_bytes=VMEM_LIMIT),
    )(place, order, own_tok, own_key, got_tok, got_key)


def input_grad_kernel(place, key, *rest):
    pieces, out = rest[:-1], rest[-1]
    step = pl.program_id(0)
    for n in range(8):
        piece = pieces[(0, 0, 1, 1, 2, 3, 4, 5)[n]]

        @pl.when(step == n)
        def _(piece=piece):
            out[...] = lax.dot_general(
                key[...], piece[...], (((1,), (1,)), ((), ())), preferred_element_type=jnp.float32
            ).astype(out.dtype)


def input_grad_of(place, key, own, core, low, high, low_core, high_core, width):
    rows = low.shape[0]
    whole = lambda i, place: (0, 0)

    def column(i, place):
        yl = lax.rem(place[0] + lax.div(i, 4), 2)
        c = lax.rem(place[1] + lax.div(lax.rem(i, 4), 2), 2)
        return 0, (yl * NC + c) * 2 + lax.rem(i, 2)

    return pl.pallas_call(
        input_grad_kernel,
        grid_spec=pltpu.PrefetchScalarGridSpec(
            num_scalar_prefetch=1,
            grid=(8,),
            in_specs=[
                pl.BlockSpec(key.shape, whole),
                pl.BlockSpec((rows, key.shape[1]), lambda i, place: (jnp.minimum(i, 1), 0)),
                pl.BlockSpec(
                    (rows, key.shape[1]), lambda i, place: (jnp.clip(i - 2, 0, 1), 0)
                ),
            ]
            + [pl.BlockSpec((rows, key.shape[1]), whole)] * 4,
            out_specs=pl.BlockSpec((key.shape[0], rows), column),
        ),
        out_shape=jax.ShapeDtypeStruct((key.shape[0], width), jnp.bfloat16),
        compiler_params=pltpu.CompilerParams(vmem_limit_bytes=VMEM_LIMIT),
    )(place, key, own, core, low, high, low_core, high_core)


def place_kernel(place, order, *rest):
    parts, out = rest[:-1], rest[-1]
    x, yh, z = place[0], place[1], place[2]
    block_rows = parts[0].shape[2]
    for k in range(NX):
        from_x = lax.rem(x + NX - k, NX)
        for n in range(NYH):
            from_yh = lax.rem(yh + n, NYH)
            for m in range(NZ):
                from_z = lax.rem(z + NZ - m, NZ)
                block = order[0, (from_z * NYH + from_yh) * NX + from_x]
                start = pl.multiple_of(block * block_rows, block_rows)
                out[pl.ds(start, block_rows), :] = parts[k][n, m]


def put_in_rows(place, order, parts, rows):
    return pl.pallas_call(
        place_kernel,
        grid_spec=pltpu.PrefetchScalarGridSpec(
            num_scalar_prefetch=2,
            grid=(1,),
            in_specs=[vmem()] * len(parts),
            out_specs=vmem(),
        ),
        out_shape=jax.ShapeDtypeStruct((rows, parts[0].shape[3]), parts[0].dtype),
        compiler_params=pltpu.CompilerParams(vmem_limit_bytes=VMEM_LIMIT),
    )(place, order, *parts)


def f32(value):
    return value.astype(jnp.float32)


def on_device(
    tokens_in, key_cotangent, key_weight, master_store, first_moment, second_moment, writer
):
    yl, c, z, yh, x = (lax.axis_index(name) for name in AXES)
    y = yh * NYL + yl
    tok_rows, width = tokens_in.shape
    rows_here = key_weight.shape[0]
    block_rows = master_store.shape[0]

    with jax.named_scope("core_swap"):
        got_key = send(key_cotangent, "c", 1)
        near_order = writer
        far_order = send(writer, "yl", 1)
        summed = {}
        for far in (1, 0):
            shard = (yl ^ far) * NC
            other = lax.dynamic_slice(
                tokens_in, (0, (shard + 1 - c) * rows_here), (tok_rows, rows_here)
            )
            got_tok = send(other, "c", 1)
            place = jnp.stack([x, y, z, shard + c]).astype(jnp.int32)
            summed[far] = both_cores(
                far,
                place,
                far_order if far else near_order,
                tokens_in,
                key_cotangent,
                got_tok,
                got_key,
                block_rows,
            )

    with jax.named_scope("first_stage"):
        first = {}
        for far in (1, 0):
            parts = summed[far][:NX]
            got = [send(parts[k], "x", k) for k in range(1, NX)]
            first[far] = f32(parts[0])
            for value in got:
                first[far] = first[far] + f32(value)
        second = f32(summed[0][NX])
        got = [
            send(summed[1][NX], "y", 1),
            send(summed[1][NX + 1], "y", 3),
            send(summed[0][NX + 1], "y", 2),
        ]
        for value in got:
            second = second + f32(value)

    with jax.named_scope("second_stage"):
        out_y = {1: first[1][0], 3: first[1][1], 2: first[0][1]}
        got_y = [send(value.astype(jnp.bfloat16), "y", j) for j, value in out_y.items()]
        got_x = [send(second[k].astype(jnp.bfloat16), "x", k) for k in range(1, NX)]
        first_half = first[0][0]
        for value in got_y:
            first_half = first_half + f32(value)
        second_half = second[0]
        for value in got_x:
            second_half = second_half + f32(value)

    with jax.named_scope("weights"):
        held, first_half, second_half = lax.optimization_barrier(
            (key_weight, first_half, second_half)
        )
        low = send(held[: rows_here // 2], "y", 1)
        high = send(held[rows_here // 2 :], "y", 3)
        core = send(held, "c", 1)
        low_core, high_core = send(low, "c", 1), send(high, "c", 1)
        input_grad = input_grad_of(
            jnp.stack([yl, c]).astype(jnp.int32),
            key_cotangent,
            held,
            core,
            low,
            high,
            low_core,
            high_core,
            width,
        )

    with jax.named_scope("third_stage"):
        blocks = [jnp.concatenate([first_half[m], second_half[m]], axis=0) for m in range(NZ)]
        own_block = blocks[0]
        for value in [send(blocks[m], "z", m) for m in range(1, NZ)]:
            own_block = own_block + value

    with jax.named_scope("adam"):
        devices = NYL * NC * NZ * NYH * NX
        stored_grad = own_block * (tok_rows * devices) ** (-0.5)
        moment_one = beta_first * first_moment + (1.0 - beta_first) * stored_grad
        moment_two = beta_second * second_moment + (1.0 - beta_second) * stored_grad * stored_grad
        corrected_one = moment_one / (1.0 - beta_first**step_count)
        corrected_two = moment_two / (1.0 - beta_second**step_count)
        master_new = master_store - learn_rate * (
            corrected_one / (jnp.sqrt(corrected_two) + adam_eps) + decay_rate * master_store
        )

    with jax.named_scope("fresh_weights"):
        fresh = master_new.astype(jnp.bfloat16)
        column = jnp.stack([fresh] + [send(fresh, "z", m) for m in range(1, NZ)])
        plane = jnp.stack([column, send(column, "yh", 1)])
        parts = [plane] + [send(plane, "x", k) for k in range(1, NX)]
        place = jnp.stack([x, yh, z]).astype(jnp.int32)
        weight_new = put_in_rows(place, near_order, parts, rows_here)
    return (input_grad, master_new, moment_one, moment_two, weight_new)


def solution(mesh):
    fine = Mesh(mesh.devices.reshape(NYL, NC, NZ, NYH, NX), AXES)
    shard, every = ("yl", "c"), AXES
    in_specs = (
        P(every, None),
        P(every, None),
        P(shard, None),
        P(every, None),
        P(every, None),
        P(every, None),
        P(shard, None),
    )
    out_specs = (P(every, None),) * 4 + (P(shard, None),)
    return jax.shard_map(
        on_device, mesh=fine, in_specs=in_specs, out_specs=out_specs, check_vma=False
    )
```

```python
import functools

import jax
import jax.numpy as jnp
from jax import lax
from jax.experimental import pallas as pl
from jax.experimental.pallas import tpu as pltpu
from jax.sharding import Mesh
from jax.sharding import PartitionSpec as P

beta_first = 0.9
beta_second = 0.95
learn_rate = 0.0003
decay_rate = 0.1
adam_eps = 1e-08
step_count = 100

NYL, NC, NZ, NYH, NX = 2, 2, 8, 2, 4
NY = NYL * NYH
AXES = ("yl", "c", "z", "yh", "x")
VMEM_LIMIT = 48 * 1024 * 1024


def shift(axis, step):
    if axis == "y":
        spot = lambda y: (y % NYL) * NYH + y // NYL
        return [(spot(y), spot((y + step) % NY)) for y in range(NY)]
    size = {"x": NX, "z": NZ, "c": NC, "yl": NYL, "yh": NYH}[axis]
    return [(i, (i + step) % size) for i in range(size)]


def send(value, axis, step):
    return lax.ppermute(value, ("yl", "yh") if axis == "y" else axis, shift(axis, step))


def vmem():
    return pl.BlockSpec(memory_space=pltpu.VMEM)


def both_cores_kernel(far, place, order, own_tok, own_key, got_tok, got_key, *rest):
    outs, total = rest[:-1], rest[-1]
    x, y = place[0], place[1]
    rows, half = total.shape[0], outs[0].shape[3]
    cut = min(512, rows)
    for q in range(rows // cut):
        piece = slice(q * cut, (q + 1) * cut)

        def partial(tok, key):
            value = lax.dot_general(
                tok[:, piece], key[...], (((0,), (0,)), ((), ())), preferred_element_type=jnp.float32
            )
            return value.astype(jnp.bfloat16).astype(jnp.float32)

        total[piece, :] = partial(own_tok, own_key) + partial(got_tok, got_key)
    for k in range(NX):
        to_x = lax.rem(x + k, NX)
        for n, j in enumerate((1, 3) if far else (0, 2)):
            to_yh = lax.div(lax.rem(y + j, NY), NYL)
            for to_z in range(NZ):
                block = order[0, (to_z * NYH + to_yh) * NX + to_x]
                start = pl.multiple_of(block * (2 * half), 2 * half)
                first = total[pl.ds(start, half), :]
                second = total[pl.ds(start + half, half), :]
                outs[0][to_x, n, to_z] = first.astype(outs[0].dtype)
                outs[1 + n][k, to_z] = second.astype(outs[1 + n].dtype)


def both_cores(far, place, order, own_tok, own_key, got_tok, got_key, block_rows):
    rows, width = got_tok.shape[1], own_key.shape[1]
    half = block_rows // 2
    shapes = [
        jax.ShapeDtypeStruct((NX, 2, NZ, half, width), jnp.bfloat16),
        jax.ShapeDtypeStruct((NX, NZ, half, width), jnp.bfloat16 if far else jnp.float32),
        jax.ShapeDtypeStruct((NX, NZ, half, width), jnp.bfloat16),
    ]
    return pl.pallas_call(
        functools.partial(both_cores_kernel, far),
        grid_spec=pltpu.PrefetchScalarGridSpec(
            num_scalar_prefetch=2,
            grid=(1,),
            in_specs=[
                pl.BlockSpec((own_tok.shape[0], rows), lambda i, place, order: (0, place[2])),
                vmem(),
                vmem(),
                vmem(),
            ],
            out_specs=[vmem()] * len(shapes),
            scratch_shapes=[pltpu.VMEM((rows, width), jnp.float32)],
        ),
        out_shape=shapes,
        compiler_params=pltpu.CompilerParams(vmem_limit_bytes=VMEM_LIMIT),
    )(place, order, own_tok, own_key, got_tok, got_key)


def input_grad_kernel(place, key, *rest):
    pieces, out = rest[:-1], rest[-1]
    step = pl.program_id(0)
    for n in range(8):
        piece = pieces[(0, 0, 1, 1, 2, 3, 4, 5)[n]]

        @pl.when(step == n)
        def _(piece=piece):
            out[...] = lax.dot_general(
                key[...], piece[...], (((1,), (1,)), ((), ())), preferred_element_type=jnp.float32
            ).astype(out.dtype)


def input_grad_of(place, key, own, core, low, high, low_core, high_core, width):
    rows = low.shape[0]
    whole = lambda i, place: (0, 0)

    def column(i, place):
        yl = lax.rem(place[0] + lax.div(i, 4), 2)
        c = lax.rem(place[1] + lax.div(lax.rem(i, 4), 2), 2)
        return 0, (yl * NC + c) * 2 + lax.rem(i, 2)

    return pl.pallas_call(
        input_grad_kernel,
        grid_spec=pltpu.PrefetchScalarGridSpec(
            num_scalar_prefetch=1,
            grid=(8,),
            in_specs=[
                pl.BlockSpec(key.shape, whole),
                pl.BlockSpec((rows, key.shape[1]), lambda i, place: (jnp.minimum(i, 1), 0)),
                pl.BlockSpec(
                    (rows, key.shape[1]), lambda i, place: (jnp.clip(i - 2, 0, 1), 0)
                ),
            ]
            + [pl.BlockSpec((rows, key.shape[1]), whole)] * 4,
            out_specs=pl.BlockSpec((key.shape[0], rows), column),
        ),
        out_shape=jax.ShapeDtypeStruct((key.shape[0], width), jnp.bfloat16),
        compiler_params=pltpu.CompilerParams(vmem_limit_bytes=VMEM_LIMIT),
    )(place, key, own, core, low, high, low_core, high_core)


def place_kernel(place, order, *rest):
    parts, out = rest[:-1], rest[-1]
    x = place[0]
    block_rows = parts[0].shape[1]
    for k in range(NX):
        from_x = lax.rem(x + NX - k, NX)
        for n in range(NZ * NYH):
            start = pl.multiple_of(order[0, n * NX + from_x] * block_rows, block_rows)
            out[pl.ds(start, block_rows), :] = parts[k][n]


def put_in_rows(place, order, parts, rows):
    return pl.pallas_call(
        place_kernel,
        grid_spec=pltpu.PrefetchScalarGridSpec(
            num_scalar_prefetch=2,
            grid=(1,),
            in_specs=[vmem()] * len(parts),
            out_specs=vmem(),
        ),
        out_shape=jax.ShapeDtypeStruct((rows, parts[0].shape[2]), parts[0].dtype),
        compiler_params=pltpu.CompilerParams(vmem_limit_bytes=VMEM_LIMIT),
    )(place, order, *parts)


def f32(value):
    return value.astype(jnp.float32)


def on_device(
    tokens_in, key_cotangent, key_weight, master_store, first_moment, second_moment, writer
):
    yl, c, z, yh, x = (lax.axis_index(name) for name in AXES)
    y = yh * NYL + yl
    tok_rows, width = tokens_in.shape
    rows_here = key_weight.shape[0]
    block_rows = master_store.shape[0]

    with jax.named_scope("core_swap"):
        got_key = send(key_cotangent, "c", 1)
        order = {0: writer, 1: send(writer, "yl", 1)}
        summed = {}
        for far in (1, 0):
            shard = (yl ^ far) * NC
            other = lax.dynamic_slice(
                tokens_in, (0, (shard + 1 - c) * rows_here), (tok_rows, rows_here)
            )
            got_tok = send(other, "c", 1)
            place = jnp.stack([x, y, shard + c]).astype(jnp.int32)
            summed[far] = both_cores(
                far,
                place,
                order[far],
                tokens_in,
                key_cotangent,
                got_tok,
                got_key,
                block_rows,
            )

    with jax.named_scope("weights"):
        low = send(key_weight[: rows_here // 2], "y", 1)
        high = send(key_weight[rows_here // 2 :], "y", 3)
        core = send(key_weight, "c", 1)
        low_core, high_core = send(low, "c", 1), send(high, "c", 1)

    with jax.named_scope("first_stage"):
        got = [
            send(summed[1][1], "y", 1),
            send(summed[1][2], "y", 3),
            send(summed[0][2], "y", 2),
        ]
        first = {}
        for far in (1, 0):
            parts = lax.all_to_all(summed[far][0], "x", 0, 0, tiled=True)
            first[far] = f32(parts[0])
            for k in range(1, NX):
                first[far] = first[far] + f32(parts[k])
        second = summed[0][1]
        for value in got:
            second = second + f32(value)

    with jax.named_scope("second_stage"):
        out_y = {1: first[1][0], 3: first[1][1], 2: first[0][1]}
        got_y = [send(value.astype(jnp.bfloat16), "y", j) for j, value in out_y.items()]
        got_x = [send(second[k].astype(jnp.bfloat16), "x", k) for k in range(1, NX)]
        first_half = first[0][0]
        for value in got_y:
            first_half = first_half + f32(value)
        second_half = second[0]
        for value in got_x:
            second_half = second_half + f32(value)

    with jax.named_scope("third_stage"):
        blocks = jnp.concatenate([first_half, second_half], axis=1)
        parts = lax.all_to_all(blocks, "z", 0, 0, tiled=True)
        own_block = jnp.sum(parts, axis=0)

    with jax.named_scope("adam"):
        devices = NYL * NC * NZ * NYH * NX
        stored_grad = own_block * (tok_rows * devices) ** (-0.5)
        moment_one = beta_first * first_moment + (1.0 - beta_first) * stored_grad
        moment_two = beta_second * second_moment + (1.0 - beta_second) * stored_grad * stored_grad
        corrected_one = moment_one / (1.0 - beta_first**step_count)
        corrected_two = moment_two / (1.0 - beta_second**step_count)
        master_new = master_store - learn_rate * (
            corrected_one / (jnp.sqrt(corrected_two) + adam_eps) + decay_rate * master_store
        )

    with jax.named_scope("fresh_weights"):
        fresh = jnp.broadcast_to(
            master_new.astype(jnp.bfloat16), (NZ * NYH,) + master_new.shape
        )
        plane = lax.all_to_all(fresh, ("z", "yh"), 0, 0, tiled=True)
        parts = [plane] + [send(plane, "x", k) for k in range(1, NX)]
        place = jnp.stack([x]).astype(jnp.int32)
        weight_new = put_in_rows(place, writer, parts, rows_here)

    with jax.named_scope("input_grad"):
        held, core, low, high, low_core, high_core, _ = lax.optimization_barrier(
            (key_weight, core, low, high, low_core, high_core, plane)
        )
        place = jnp.stack([yl, c]).astype(jnp.int32)
        input_grad = input_grad_of(
            place, key_cotangent, held, core, low, high, low_core, high_core, width
        )
    return (input_grad, master_new, moment_one, moment_two, weight_new)


def solution(mesh):
    fine = Mesh(mesh.devices.reshape(NYL, NC, NZ, NYH, NX), AXES)
    shard, every = ("yl", "c"), AXES
    in_specs = (
        P(every, None),
        P(every, None),
        P(shard, None),
        P(every, None),
        P(every, None),
        P(every, None),
        P(shard, None),
    )
    out_specs = (P(every, None),) * 4 + (P(shard, None),)
    return jax.shard_map(
        on_device, mesh=fine, in_specs=in_specs, out_specs=out_specs, check_vma=False
    )
```

```python
import functools

import jax
import jax.numpy as jnp
from jax import lax
from jax.experimental import pallas as pl
from jax.experimental.pallas import tpu as pltpu
from jax.sharding import Mesh
from jax.sharding import PartitionSpec as P

beta_first = 0.9
beta_second = 0.95
learn_rate = 0.0003
decay_rate = 0.1
adam_eps = 1e-08
step_count = 100

NYL, NC, NZ, NYH, NX = 2, 2, 8, 2, 4
NY = NYL * NYH
AXES = ("yl", "c", "z", "yh", "x")
MIB = 1024 * 1024


def shift(axis, step):
    if axis == "y":
        spot = lambda y: (y % NYL) * NYH + y // NYL
        return [(spot(y), spot((y + step) % NY)) for y in range(NY)]
    size = {"x": NX, "z": NZ, "c": NC, "yl": NYL, "yh": NYH}[axis]
    return [(i, (i + step) % size) for i in range(size)]


def send(value, axis, step):
    return lax.ppermute(value, ("yl", "yh") if axis == "y" else axis, shift(axis, step))


def vmem():
    return pl.BlockSpec(memory_space=pltpu.VMEM)


def spec(block, index):
    return pl.BlockSpec(block, index)


def params(mib):
    return pltpu.CompilerParams(vmem_limit_bytes=mib * MIB)


def columns_kernel(place, tokens, far, near, sems):
    copies = []
    for n, out in enumerate((far, near)):
        rows = out.shape[1]
        start = pl.multiple_of(place[n] * rows, rows)
        copies.append(pltpu.make_async_copy(tokens.at[:, pl.ds(start, rows)], out, sems.at[n]))
    for copy in copies:
        copy.start()
    for copy in copies:
        copy.wait()


def columns_of(place, tokens, rows):
    shape = jax.ShapeDtypeStruct((tokens.shape[0], rows), tokens.dtype)
    return pl.pallas_call(
        columns_kernel,
        grid_spec=pltpu.PrefetchScalarGridSpec(
            num_scalar_prefetch=1,
            grid=(1,),
            in_specs=[pl.BlockSpec(memory_space=pl.ANY)],
            out_specs=[pl.BlockSpec(memory_space=pl.ANY)] * 2,
            scratch_shapes=[pltpu.SemaphoreType.DMA((2,))],
        ),
        out_shape=[shape, shape],
        compiler_params=params(6),
    )(place, pltpu.with_memory_space_constraint(tokens, pltpu.HBM))


def partial_of(tok, key):
    value = lax.dot_general(tok, key, (((0,), (0,)), ((), ())), preferred_element_type=jnp.float32)
    return value.astype(jnp.bfloat16)


def own_kernel(place, tok, key, out):
    out[0] = partial_of(tok[...], key[...])


def own_partials(place, tokens, key, rows):
    cut = min(512, rows)
    steps = rows // cut
    return pl.pallas_call(
        own_kernel,
        grid_spec=pltpu.PrefetchScalarGridSpec(
            num_scalar_prefetch=1,
            grid=(2, steps),
            in_specs=[
                spec((tokens.shape[0], cut), lambda n, q, place: (0, place[n] * steps + q)),
                spec(key.shape, lambda n, q, place: (0, 0)),
            ],
            out_specs=spec((1, cut, key.shape[1]), lambda n, q, place: (n, q, 0)),
        ),
        out_shape=jax.ShapeDtypeStruct((2, rows, key.shape[1]), jnp.bfloat16),
        compiler_params=params(8),
    )(place, pltpu.with_memory_space_constraint(tokens, pltpu.HBM), key)


def both_cores_kernel(place, far_order, near_order, own, far, near, key, *rest):
    by_x, by_y, total = rest[:NX], rest[NX : NX + NY], rest[-1]
    x, y = place[0], place[1]
    rows, half = total.shape[0], by_x[0].shape[2]
    cut = min(512, rows)
    for s, (tok, order) in enumerate(((far, far_order), (near, near_order))):
        for q in range(rows // cut):
            piece = slice(q * cut, (q + 1) * cut)
            got = partial_of(tok[:, piece], key[...])
            total[piece, :] = own[s, piece, :].astype(jnp.float32) + got.astype(jnp.float32)
        for j in (1 - s, 3 - s):
            to_yh = lax.div(lax.rem(y + j, NY), NYL)
            for k in range(NX):
                to_x = lax.rem(x + k, NX)
                for to_z in range(NZ):
                    block = order[0, (to_z * NYH + to_yh) * NX + to_x]
                    start = pl.multiple_of(block * (2 * half), 2 * half)
                    first = total[pl.ds(start, half), :]
                    second = total[pl.ds(start + half, half), :]
                    by_x[k][j, to_z] = first.astype(by_x[k].dtype)
                    by_y[j][k, to_z] = second.astype(by_y[j].dtype)


def both_cores(place, far_order, near_order, own, far, near, key, block_rows):
    rows, width = own.shape[1], own.shape[2]
    half = block_rows // 2
    shapes = [
        jax.ShapeDtypeStruct((count, NZ, half, width), jnp.bfloat16 if n else jnp.float32)
        for count, steps in ((NY, NX), (NX, NY))
        for n in range(steps)
    ]
    return pl.pallas_call(
        both_cores_kernel,
        grid_spec=pltpu.PrefetchScalarGridSpec(
            num_scalar_prefetch=3,
            grid=(1,),
            in_specs=[vmem()] * 4,
            out_specs=[vmem()] * len(shapes),
            scratch_shapes=[pltpu.VMEM((rows, width), jnp.float32)],
        ),
        out_shape=shapes,
        compiler_params=params(20),
    )(place, far_order, near_order, own, far, near, key)


def input_grad_kernel(place, key, weight, *rest):
    out = rest[-1]
    out[...] = lax.dot_general(
        key[...], weight[...], (((1,), (1,)), ((), ())), preferred_element_type=jnp.float32
    ).astype(out.dtype)


def input_grad_of(place, key, weight, width, before=None):
    cut = weight.shape[0] // 4
    extra = [] if before is None else [before]
    return pl.pallas_call(
        input_grad_kernel,
        grid_spec=pltpu.PrefetchScalarGridSpec(
            num_scalar_prefetch=1,
            grid=(4,),
            in_specs=[
                spec(key.shape, lambda i, place: (0, 0)),
                spec((cut, key.shape[1]), lambda i, place: (i, 0)),
            ]
            + [pl.BlockSpec(memory_space=pl.ANY)] * len(extra),
            out_specs=spec(
                (key.shape[0], cut),
                lambda i, place: (0, (lax.div(i, 2) * NC + place[0]) * 2 + lax.rem(i, 2)),
            ),
        ),
        out_shape=jax.ShapeDtypeStruct((key.shape[0], width), jnp.bfloat16),
        input_output_aliases={3: 0} if extra else {},
        compiler_params=params(10),
    )(place, key, weight, *extra)


def place_kernel(place, order, *rest):
    parts, out = rest[:-1], rest[-1]
    x = place[0]
    block_rows = parts[0].shape[1]
    for k in range(NX):
        from_x = lax.rem(x + NX - k, NX)
        for n in range(NZ * NYH):
            start = pl.multiple_of(order[0, n * NX + from_x] * block_rows, block_rows)
            out[pl.ds(start, block_rows), :] = parts[k][n]


def put_in_rows(place, order, parts, rows):
    return pl.pallas_call(
        place_kernel,
        grid_spec=pltpu.PrefetchScalarGridSpec(
            num_scalar_prefetch=2,
            grid=(1,),
            in_specs=[vmem()] * len(parts),
            out_specs=vmem(),
        ),
        out_shape=jax.ShapeDtypeStruct((rows, parts[0].shape[2]), parts[0].dtype),
        compiler_params=params(8),
    )(place, order, *parts)


def f32(value):
    return value.astype(jnp.float32)


def total_of(values):
    total = f32(values[0])
    for value in values[1:]:
        total = total + f32(value)
    return total


def on_device(
    tokens_in, key_cotangent, key_weight, master_store, first_moment, second_moment, writer
):
    yl, c, _, yh, x = (lax.axis_index(name) for name in AXES)
    tok_rows, width = tokens_in.shape
    rows_here = key_weight.shape[0]
    block_rows = master_store.shape[0]

    with jax.named_scope("core_swap"):
        here, there = yl * NC, (1 - yl) * NC
        got_key = send(key_cotangent, "c", 1)
        far_order = send(writer, "yl", 1)
        far, near = columns_of(
            jnp.stack([there + 1 - c, here + 1 - c]).astype(jnp.int32), tokens_in, rows_here
        )
        far, near = send(far, "c", 1), send(near, "c", 1)
        own = own_partials(
            jnp.stack([there + c, here + c]).astype(jnp.int32), tokens_in, key_cotangent, rows_here
        )
        place = jnp.stack([x, yh * NYL + yl]).astype(jnp.int32)
        parts = both_cores(place, far_order, writer, own, far, near, got_key, block_rows)
        by_x, by_y = list(parts[:NX]), list(parts[NX:])

    def sums(parts):
        values = [total_of([part[n] for part in parts]) for n in range(parts[0].shape[0])]
        return values[:1] + [value.astype(jnp.bfloat16) for value in values[1:]]

    with jax.named_scope("first_stage"):
        second = sums(by_y[:1] + [send(by_y[j], "y", j) for j in (1, 3, 2)])
        first = sums(by_x[:1] + [send(by_x[k], "x", k) for k in (1, 3, 2)])

    with jax.named_scope("weights"):
        held, first, second = lax.optimization_barrier((key_weight, first, second))
        column = lax.all_gather(held, "yl", axis=0, tiled=True)

    with jax.named_scope("second_stage"):
        second_half = total_of(second[:1] + [send(second[k], "x", k) for k in range(1, NX)])
        first_half = total_of(first[:1] + [send(first[j], "y", j) for j in range(1, NY)])

    with jax.named_scope("third_stage"):
        blocks = jnp.concatenate([first_half, second_half], axis=1)
        parts = lax.all_to_all(blocks, "z", 0, 0, tiled=True)
        own_block = jnp.sum(parts, axis=0)

    with jax.named_scope("adam"):
        devices = NYL * NC * NZ * NYH * NX
        stored_grad = own_block * (tok_rows * devices) ** (-0.5)
        moment_one = beta_first * first_moment + (1.0 - beta_first) * stored_grad
        moment_two = beta_second * second_moment + (1.0 - beta_second) * stored_grad * stored_grad
        corrected_one = moment_one / (1.0 - beta_first**step_count)
        corrected_two = moment_two / (1.0 - beta_second**step_count)
        master_new = master_store - learn_rate * (
            corrected_one / (jnp.sqrt(corrected_two) + adam_eps) + decay_rate * master_store
        )

    with jax.named_scope("fresh_weights"):
        fresh = jnp.broadcast_to(
            master_new.astype(jnp.bfloat16), (NZ * NYH,) + master_new.shape
        )
        plane = lax.all_to_all(fresh, ("z", "yh"), 0, 0, tiled=True)
        parts = [plane] + [send(plane, "x", k) for k in range(1, NX)]

    with jax.named_scope("input_grad"):
        column, _ = lax.optimization_barrier((column, plane))
        other = send(column, "c", 1)
        core = jnp.stack([c]).astype(jnp.int32)
        held = pltpu.with_memory_space_constraint(column, pltpu.HBM)
        input_grad = input_grad_of(core, key_cotangent, held, width)
        input_grad = input_grad_of(1 - core, key_cotangent, other, width, input_grad)

    with jax.named_scope("rows"):
        input_grad, *parts = lax.optimization_barrier((input_grad, *parts))
        place = jnp.stack([x]).astype(jnp.int32)
        weight_new = put_in_rows(place, writer, parts, rows_here)
    return (input_grad, master_new, moment_one, moment_two, weight_new)


def solution(mesh):
    fine = Mesh(mesh.devices.reshape(NYL, NC, NZ, NYH, NX), AXES)
    shard, every = ("yl", "c"), AXES
    in_specs = (
        P(every, None),
        P(every, None),
        P(shard, None),
        P(every, None),
        P(every, None),
        P(every, None),
        P(shard, None),
    )
    out_specs = (P(every, None),) * 4 + (P(shard, None),)
    return jax.shard_map(
        on_device, mesh=fine, in_specs=in_specs, out_specs=out_specs, check_vma=False
    )
```

```python
import functools

import jax
import jax.numpy as jnp
from jax import lax
from jax.experimental import pallas as pl
from jax.experimental.pallas import tpu as pltpu
from jax.sharding import Mesh
from jax.sharding import PartitionSpec as P

beta_first = 0.9
beta_second = 0.95
learn_rate = 0.0003
decay_rate = 0.1
adam_eps = 1e-08
step_count = 100

NYL, NC, NZ, NYH, NX = 2, 2, 8, 2, 4
NY = NYL * NYH
AXES = ("yl", "c", "z", "yh", "x")
MIB = 1024 * 1024


def shift(axis, step):
    if axis == "y":
        spot = lambda y: (y % NYL) * NYH + y // NYL
        return [(spot(y), spot((y + step) % NY)) for y in range(NY)]
    size = {"x": NX, "z": NZ, "c": NC, "yl": NYL, "yh": NYH}[axis]
    return [(i, (i + step) % size) for i in range(size)]


def send(value, axis, step):
    return lax.ppermute(value, ("yl", "yh") if axis == "y" else axis, shift(axis, step))


def cross(value):
    pairs = []
    for y in range(NY):
        for c in range(NC):
            to = (y + 1 + 2 * c) % NY
            pairs.append(tuple(((n % NYL) * NC + c) * NYH + n // NYL for n in (y, to)))
    return lax.ppermute(value, ("yl", "c", "yh"), pairs)


def vmem():
    return pl.BlockSpec(memory_space=pltpu.VMEM)


def spec(block, index):
    return pl.BlockSpec(block, index)


def params(mib):
    return pltpu.CompilerParams(vmem_limit_bytes=mib * MIB)


def columns_kernel(place, tokens, far, near, sems):
    copies = []
    for n, out in enumerate((far, near)):
        rows = out.shape[1]
        start = pl.multiple_of(place[n] * rows, rows)
        copies.append(pltpu.make_async_copy(tokens.at[:, pl.ds(start, rows)], out, sems.at[n]))
    for copy in copies:
        copy.start()
    for copy in copies:
        copy.wait()


def columns_of(place, tokens, rows):
    shape = jax.ShapeDtypeStruct((tokens.shape[0], rows), tokens.dtype)
    return pl.pallas_call(
        columns_kernel,
        grid_spec=pltpu.PrefetchScalarGridSpec(
            num_scalar_prefetch=1,
            grid=(1,),
            in_specs=[pl.BlockSpec(memory_space=pl.ANY)],
            out_specs=[vmem(), vmem()],
            scratch_shapes=[pltpu.SemaphoreType.DMA((2,))],
        ),
        out_shape=[shape, shape],
        compiler_params=params(6),
    )(place, pltpu.with_memory_space_constraint(tokens, pltpu.HBM))


def partial_of(tok, key):
    value = lax.dot_general(tok, key, (((0,), (0,)), ((), ())), preferred_element_type=jnp.float32)
    return value.astype(jnp.bfloat16)


def own_kernel(place, tok, key, out):
    out[0] = partial_of(tok[...], key[...])


def own_partials(place, tokens, key, rows):
    cut = min(1024, rows)
    steps = rows // cut
    return pl.pallas_call(
        own_kernel,
        grid_spec=pltpu.PrefetchScalarGridSpec(
            num_scalar_prefetch=1,
            grid=(2, steps),
            in_specs=[
                spec((tokens.shape[0], cut), lambda n, q, place: (0, place[n] * steps + q)),
                spec(key.shape, lambda n, q, place: (0, 0)),
            ],
            out_specs=spec((1, cut, key.shape[1]), lambda n, q, place: (n, q, 0)),
        ),
        out_shape=jax.ShapeDtypeStruct((2, rows, key.shape[1]), jnp.bfloat16),
        compiler_params=params(8),
    )(place, pltpu.with_memory_space_constraint(tokens, pltpu.HBM), key)


def both_cores_kernel(place, far_order, near_order, own, far, near, key, *rest):
    by_x, by_y, total = rest[:NX], rest[NX : NX + NY], rest[-1]
    x, y = place[0], place[1]
    rows, half = total.shape[0], by_x[0].shape[2]
    cut = min(512, rows)
    for s, (tok, order) in enumerate(((far, far_order), (near, near_order))):
        for q in range(rows // cut):
            piece = slice(q * cut, (q + 1) * cut)
            got = partial_of(tok[:, piece], key[...])
            total[piece, :] = own[s, piece, :].astype(jnp.float32) + got.astype(jnp.float32)
        for j in (1 - s, 3 - s):
            to_yh = lax.div(lax.rem(y + j, NY), NYL)
            for k in range(NX):
                to_x = lax.rem(x + k, NX)
                for to_z in range(NZ):
                    block = order[0, (to_z * NYH + to_yh) * NX + to_x]
                    start = pl.multiple_of(block * (2 * half), 2 * half)
                    first = total[pl.ds(start, half), :]
                    second = total[pl.ds(start + half, half), :]
                    by_x[k][j, to_z] = first.astype(by_x[k].dtype)
                    by_y[j][k, to_z] = second.astype(by_y[j].dtype)


def both_cores(place, far_order, near_order, own, far, near, key, block_rows):
    rows, width = own.shape[1], own.shape[2]
    half = block_rows // 2
    shapes = [
        jax.ShapeDtypeStruct((count, NZ, half, width), jnp.bfloat16 if n else jnp.float32)
        for count, steps in ((NY, NX), (NX, NY))
        for n in range(steps)
    ]
    return pl.pallas_call(
        both_cores_kernel,
        grid_spec=pltpu.PrefetchScalarGridSpec(
            num_scalar_prefetch=3,
            grid=(1,),
            in_specs=[vmem()] * 4,
            out_specs=[vmem()] * len(shapes),
            scratch_shapes=[pltpu.VMEM((rows, width), jnp.float32)],
        ),
        out_shape=shapes,
        compiler_params=params(20),
    )(place, far_order, near_order, own, far, near, key)


def input_grad_kernel(place, key, first, second, *rest):
    out = rest[-1]
    for n, weight in enumerate((first, second)):

        @pl.when(lax.div(pl.program_id(0), 2) == n)
        def _(weight=weight):
            out[...] = lax.dot_general(
                key[...], weight[...], (((1,), (1,)), ((), ())), preferred_element_type=jnp.float32
            ).astype(out.dtype)


def input_grad_of(place, key, first, second, width, before=None):
    cut = first.shape[0] // 2
    extra = [] if before is None else [before]
    return pl.pallas_call(
        input_grad_kernel,
        grid_spec=pltpu.PrefetchScalarGridSpec(
            num_scalar_prefetch=1,
            grid=(4,),
            in_specs=[
                spec(key.shape, lambda i, place: (0, 0)),
                spec((cut, key.shape[1]), lambda i, place: (jnp.minimum(i, 1), 0)),
                spec((cut, key.shape[1]), lambda i, place: (jnp.maximum(i - 2, 0), 0)),
            ]
            + [pl.BlockSpec(memory_space=pl.ANY)] * len(extra),
            out_specs=spec(
                (key.shape[0], cut),
                lambda i, place: (0, place[lax.div(i, 2)] * 2 + lax.rem(i, 2)),
            ),
        ),
        out_shape=jax.ShapeDtypeStruct((key.shape[0], width), jnp.bfloat16),
        input_output_aliases={4: 0} if extra else {},
        compiler_params=params(12),
    )(place, key, first, second, *extra)


def rows_kernel(steps, place, order, *rest):
    parts, out, sems = rest[: len(steps)], rest[-2], rest[-1]
    x = place[0]
    block_rows = parts[0].shape[1]
    copies = []
    for i, k in enumerate(steps):
        from_x = lax.rem(x + NX - k, NX)
        for n in range(NZ * NYH):
            start = pl.multiple_of(order[0, n * NX + from_x] * block_rows, block_rows)
            copies.append(
                pltpu.make_async_copy(
                    parts[i].at[n], out.at[pl.ds(start, block_rows), :], sems.at[i, n]
                )
            )
    for copy in copies:
        copy.start()
    for copy in copies:
        copy.wait()


def put_in_rows(place, order, parts, rows, before=None):
    steps, values = tuple(parts), list(parts.values())
    extra = [] if before is None else [before]
    return pl.pallas_call(
        functools.partial(rows_kernel, steps),
        grid_spec=pltpu.PrefetchScalarGridSpec(
            num_scalar_prefetch=2,
            grid=(1,),
            in_specs=[vmem()] * len(values) + [pl.BlockSpec(memory_space=pl.ANY)] * len(extra),
            out_specs=pl.BlockSpec(memory_space=pl.ANY),
            scratch_shapes=[pltpu.SemaphoreType.DMA((len(steps), NZ * NYH))],
        ),
        out_shape=jax.ShapeDtypeStruct((rows, values[0].shape[2]), values[0].dtype),
        input_output_aliases={2 + len(values): 0} if extra else {},
        compiler_params=params(6),
    )(place, order, *values, *extra)


def f32(value):
    return value.astype(jnp.float32)


def total_of(values):
    total = f32(values[0])
    for value in values[1:]:
        total = total + f32(value)
    return total


def on_device(
    tokens_in, key_cotangent, key_weight, master_store, first_moment, second_moment, writer
):
    yl, c, _, yh, x = (lax.axis_index(name) for name in AXES)
    tok_rows, width = tokens_in.shape
    rows_here = key_weight.shape[0]
    block_rows = master_store.shape[0]

    with jax.named_scope("core_swap"):
        here, there = yl * NC, (1 - yl) * NC
        got_key = send(key_cotangent, "c", 1)
        far_order = send(writer, "yl", 1)
        far, near = columns_of(
            jnp.stack([there + 1 - c, here + 1 - c]).astype(jnp.int32), tokens_in, rows_here
        )
        far, near = send(far, "c", 1), send(near, "c", 1)
        own = own_partials(
            jnp.stack([there + c, here + c]).astype(jnp.int32), tokens_in, key_cotangent, rows_here
        )
        place = jnp.stack([x, yh * NYL + yl]).astype(jnp.int32)
        parts = both_cores(place, far_order, writer, own, far, near, got_key, block_rows)
        by_x, by_y = list(parts[:NX]), list(parts[NX:])

    def sums(parts):
        values = [total_of([part[n] for part in parts]) for n in range(parts[0].shape[0])]
        return values[:1] + [value.astype(jnp.bfloat16) for value in values[1:]]

    def exchange(over_x, over_y):
        steps = [("x", 1), ("y", 1), ("y", 2), ("y", 3), ("x", 3), ("x", 2)]
        values = [send((over_x if axis == "x" else over_y)[n], axis, n) for axis, n in steps]
        got = dict(zip(steps, lax.optimization_barrier(values)))
        got_x = [over_x[0]] + [got["x", k] for k in range(1, NX)]
        got_y = [over_y[0]] + [got["y", j] for j in range(1, NY)]
        return got_x, got_y

    with jax.named_scope("first_stage"):
        first, second = (sums(got) for got in exchange(by_x, by_y))

    with jax.named_scope("second_stage"):
        second_half, first_half = (total_of(got) for got in exchange(second, first))
        blocks = jnp.concatenate([first_half, second_half], axis=1)

    with jax.named_scope("weights"):
        core = send(key_weight, "c", 1)
        held, blocks = lax.optimization_barrier((key_weight, blocks))
        other = cross(held)

    with jax.named_scope("third_stage"):
        parts = lax.all_to_all(blocks, "z", 0, 0, tiled=True)
        own_block = total_of([parts[n] for n in range(NZ)])

    with jax.named_scope("adam"):
        devices = NYL * NC * NZ * NYH * NX
        stored_grad = own_block * (tok_rows * devices) ** (-0.5)
        moment_one = beta_first * first_moment + (1.0 - beta_first) * stored_grad
        moment_two = beta_second * second_moment + (1.0 - beta_second) * stored_grad * stored_grad
        corrected_one = moment_one / (1.0 - beta_first**step_count)
        corrected_two = moment_two / (1.0 - beta_second**step_count)
        master_new = master_store - learn_rate * (
            corrected_one / (jnp.sqrt(corrected_two) + adam_eps) + decay_rate * master_store
        )

    with jax.named_scope("fresh_weights"):
        fresh = jnp.broadcast_to(
            master_new.astype(jnp.bfloat16), (NZ * NYH,) + master_new.shape
        )
        plane = lax.all_to_all(fresh, ("z", "yh"), 0, 0, tiled=True)
        parts = {k: send(plane, "x", k) for k in (1, 3, 2)}

    with jax.named_scope("input_grad"):
        place = jnp.stack([here + c, here + 1 - c]).astype(jnp.int32)
        input_grad = input_grad_of(place, key_cotangent, key_weight, core, width)
        other, _ = lax.optimization_barrier((other, plane))
        other_core = send(other, "c", 1)
        place = jnp.stack([there + c, there + 1 - c]).astype(jnp.int32)
        input_grad = input_grad_of(place, key_cotangent, other, other_core, width, input_grad)

    with jax.named_scope("rows"):
        last = {2: parts.pop(2)}
        parts, input_grad = lax.optimization_barrier(({0: plane} | parts, input_grad))
        place = jnp.stack([x]).astype(jnp.int32)
        weight_new = put_in_rows(place, writer, parts, rows_here)
        weight_new = put_in_rows(place, writer, last, rows_here, weight_new)
    return (input_grad, master_new, moment_one, moment_two, weight_new)


def solution(mesh):
    fine = Mesh(mesh.devices.reshape(NYL, NC, NZ, NYH, NX), AXES)
    shard, every = ("yl", "c"), AXES
    in_specs = (
        P(every, None),
        P(every, None),
        P(shard, None),
        P(every, None),
        P(every, None),
        P(every, None),
        P(shard, None),
    )
    out_specs = (P(every, None),) * 4 + (P(shard, None),)
    return jax.shard_map(
        on_device, mesh=fine, in_specs=in_specs, out_specs=out_specs, check_vma=False
    )
```

```python
import functools

import jax
import jax.numpy as jnp
from jax import lax
from jax.experimental import pallas as pl
from jax.experimental.pallas import tpu as pltpu
from jax.sharding import Mesh
from jax.sharding import PartitionSpec as P

beta_first = 0.9
beta_second = 0.95
learn_rate = 0.0003
decay_rate = 0.1
adam_eps = 1e-08
step_count = 100

NYL, NC, NZ, NYH, NX = 2, 2, 8, 2, 4
NY = NYL * NYH
AXES = ("yl", "c", "z", "yh", "x")
MIB = 1024 * 1024


def shift(axis, step):
    if axis == "y":
        spot = lambda y: (y % NYL) * NYH + y // NYL
        return [(spot(y), spot((y + step) % NY)) for y in range(NY)]
    size = {"x": NX, "z": NZ, "c": NC, "yl": NYL, "yh": NYH}[axis]
    return [(i, (i + step) % size) for i in range(size)]


def send(value, axis, step):
    return lax.ppermute(value, ("yl", "yh") if axis == "y" else axis, shift(axis, step))


def cross(value):
    pairs = []
    for y in range(NY):
        for c in range(NC):
            to = (y + 1 + 2 * c) % NY
            pairs.append(tuple(((n % NYL) * NC + c) * NYH + n // NYL for n in (y, to)))
    return lax.ppermute(value, ("yl", "c", "yh"), pairs)


def vmem():
    return pl.BlockSpec(memory_space=pltpu.VMEM)


def spec(block, index):
    return pl.BlockSpec(block, index)


def params(mib):
    return pltpu.CompilerParams(vmem_limit_bytes=mib * MIB)


def columns_kernel(place, tokens, far, near, sems):
    copies = []
    for n, out in enumerate((far, near)):
        rows = out.shape[1]
        start = pl.multiple_of(place[n] * rows, rows)
        copies.append(pltpu.make_async_copy(tokens.at[:, pl.ds(start, rows)], out, sems.at[n]))
    for copy in copies:
        copy.start()
    for copy in copies:
        copy.wait()


def columns_of(place, tokens, rows):
    shape = jax.ShapeDtypeStruct((tokens.shape[0], rows), tokens.dtype)
    return pl.pallas_call(
        columns_kernel,
        grid_spec=pltpu.PrefetchScalarGridSpec(
            num_scalar_prefetch=1,
            grid=(1,),
            in_specs=[pl.BlockSpec(memory_space=pl.ANY)],
            out_specs=[vmem(), vmem()],
            scratch_shapes=[pltpu.SemaphoreType.DMA((2,))],
        ),
        out_shape=[shape, shape],
        compiler_params=params(6),
    )(place, pltpu.with_memory_space_constraint(tokens, pltpu.HBM))


def partial_of(tok, key):
    value = lax.dot_general(tok, key, (((0,), (0,)), ((), ())), preferred_element_type=jnp.float32)
    return value.astype(jnp.bfloat16)


def own_kernel(place, tok, key, out):
    out[0] = partial_of(tok[...], key[...])


def own_partials(place, tokens, key, rows):
    cut = min(1024, rows)
    steps = rows // cut
    return pl.pallas_call(
        own_kernel,
        grid_spec=pltpu.PrefetchScalarGridSpec(
            num_scalar_prefetch=1,
            grid=(2, steps),
            in_specs=[
                spec((tokens.shape[0], cut), lambda n, q, place: (0, place[n] * steps + q)),
                spec(key.shape, lambda n, q, place: (0, 0)),
            ],
            out_specs=spec((1, cut, key.shape[1]), lambda n, q, place: (n, q, 0)),
        ),
        out_shape=jax.ShapeDtypeStruct((2, rows, key.shape[1]), jnp.bfloat16),
        compiler_params=params(8),
    )(place, pltpu.with_memory_space_constraint(tokens, pltpu.HBM), key)


def both_cores_kernel(place, far_order, near_order, own, far, near, key, *rest):
    by_x, by_y, total = rest[:NX], rest[NX : NX + NY], rest[-1]
    x, y = place[0], place[1]
    rows, half = total.shape[0], by_x[0].shape[2]
    cut = min(512, rows)
    for s, (tok, order) in enumerate(((far, far_order), (near, near_order))):
        for q in range(rows // cut):
            piece = slice(q * cut, (q + 1) * cut)
            got = partial_of(tok[:, piece], key[...])
            total[piece, :] = own[s, piece, :].astype(jnp.float32) + got.astype(jnp.float32)
        for j in (1 - s, 3 - s):
            to_yh = lax.div(lax.rem(y + j, NY), NYL)
            for k in range(NX):
                to_x = lax.rem(x + k, NX)
                for to_z in range(NZ):
                    block = order[0, (to_z * NYH + to_yh) * NX + to_x]
                    start = pl.multiple_of(block * (2 * half), 2 * half)
                    first = total[pl.ds(start, half), :]
                    second = total[pl.ds(start + half, half), :]
                    by_x[k][j, to_z] = first.astype(by_x[k].dtype)
                    by_y[j][k, to_z] = second.astype(by_y[j].dtype)


def both_cores(place, far_order, near_order, own, far, near, key, block_rows):
    rows, width = own.shape[1], own.shape[2]
    half = block_rows // 2
    shapes = [
        jax.ShapeDtypeStruct((count, NZ, half, width), jnp.bfloat16 if n else jnp.float32)
        for count, steps in ((NY, NX), (NX, NY))
        for n in range(steps)
    ]
    return pl.pallas_call(
        both_cores_kernel,
        grid_spec=pltpu.PrefetchScalarGridSpec(
            num_scalar_prefetch=3,
            grid=(1,),
            in_specs=[vmem()] * 4,
            out_specs=[vmem()] * len(shapes),
            scratch_shapes=[pltpu.VMEM((rows, width), jnp.float32)],
        ),
        out_shape=shapes,
        compiler_params=params(20),
    )(place, far_order, near_order, own, far, near, key)


def input_grad_kernel(place, key, first, second, *rest):
    out = rest[-1]
    for n, weight in enumerate((first, second)):

        @pl.when(lax.div(pl.program_id(0), 2) == n)
        def _(weight=weight):
            out[...] = lax.dot_general(
                key[...], weight[...], (((1,), (1,)), ((), ())), preferred_element_type=jnp.float32
            ).astype(out.dtype)


def input_grad_of(place, key, first, second, width, before=None):
    cut = first.shape[0] // 2
    extra = [] if before is None else [before]
    return pl.pallas_call(
        input_grad_kernel,
        grid_spec=pltpu.PrefetchScalarGridSpec(
            num_scalar_prefetch=1,
            grid=(4,),
            in_specs=[
                spec(key.shape, lambda i, place: (0, 0)),
                spec((cut, key.shape[1]), lambda i, place: (jnp.minimum(i, 1), 0)),
                spec((cut, key.shape[1]), lambda i, place: (jnp.maximum(i - 2, 0), 0)),
            ]
            + [pl.BlockSpec(memory_space=pl.ANY)] * len(extra),
            out_specs=spec(
                (key.shape[0], cut),
                lambda i, place: (0, place[lax.div(i, 2)] * 2 + lax.rem(i, 2)),
            ),
        ),
        out_shape=jax.ShapeDtypeStruct((key.shape[0], width), jnp.bfloat16),
        input_output_aliases={4: 0} if extra else {},
        compiler_params=params(12),
    )(place, key, first, second, *extra)


def rows_kernel(steps, place, order, *rest):
    parts, out, sems = rest[: len(steps)], rest[-2], rest[-1]
    x = place[0]
    block_rows = parts[0].shape[-2]
    copies = []
    for part, k in zip(parts, steps):
        for n in range(NZ * NYH):
            for back in range(NX) if k is None else (k,):
                from_x = lax.rem(x + NX - back, NX)
                start = pl.multiple_of(order[0, n * NX + from_x] * block_rows, block_rows)
                width = part.shape[-1]
                first = out.shape[1] - width if k is None else 0
                copies.append(
                    pltpu.make_async_copy(
                        part.at[n, back] if k is None else part.at[n],
                        out.at[pl.ds(start, block_rows), first : first + width],
                        sems.at[len(copies)],
                    )
                )
    for copy in copies:
        copy.start()
    for copy in copies:
        copy.wait()


def put_in_rows(place, order, parts, shape, before=None):
    steps, values = tuple(parts), list(parts.values())
    extra = [] if before is None else [before]
    count = sum(NZ * NYH * (NX if k is None else 1) for k in steps)
    return pl.pallas_call(
        functools.partial(rows_kernel, steps),
        grid_spec=pltpu.PrefetchScalarGridSpec(
            num_scalar_prefetch=2,
            grid=(1,),
            in_specs=[vmem()] * len(values) + [pl.BlockSpec(memory_space=pl.ANY)] * len(extra),
            out_specs=pl.BlockSpec(memory_space=pl.ANY),
            scratch_shapes=[pltpu.SemaphoreType.DMA((count,))],
        ),
        out_shape=jax.ShapeDtypeStruct(shape, values[0].dtype),
        input_output_aliases={2 + len(values): 0} if extra else {},
        compiler_params=params(6),
    )(place, order, *values, *extra)


def f32(value):
    return value.astype(jnp.float32)


def total_of(values):
    total = f32(values[0])
    for value in values[1:]:
        total = total + f32(value)
    return total


def on_device(
    tokens_in, key_cotangent, key_weight, master_store, first_moment, second_moment, writer
):
    yl, c, _, yh, x = (lax.axis_index(name) for name in AXES)
    tok_rows, depth = tokens_in.shape
    width = key_weight.shape[1]
    rows_here = key_weight.shape[0]
    block_rows = master_store.shape[0]

    with jax.named_scope("core_swap"):
        here, there = yl * NC, (1 - yl) * NC
        got_key = send(key_cotangent, "c", 1)
        far_order = send(writer, "yl", 1)
        far, near = columns_of(
            jnp.stack([there + 1 - c, here + 1 - c]).astype(jnp.int32), tokens_in, rows_here
        )
        far, near = send(far, "c", 1), send(near, "c", 1)
        own = own_partials(
            jnp.stack([there + c, here + c]).astype(jnp.int32), tokens_in, key_cotangent, rows_here
        )
        place = jnp.stack([x, yh * NYL + yl]).astype(jnp.int32)
        parts = both_cores(place, far_order, writer, own, far, near, got_key, block_rows)
        by_x, by_y = list(parts[:NX]), list(parts[NX:])

    def sums(parts):
        values = [total_of([part[n] for part in parts]) for n in range(parts[0].shape[0])]
        return values[:1] + [value.astype(jnp.bfloat16) for value in values[1:]]

    def exchange(over_x, over_y):
        steps = [("x", 1), ("y", 1), ("y", 2), ("y", 3), ("x", 3), ("x", 2)]
        values = [send((over_x if axis == "x" else over_y)[n], axis, n) for axis, n in steps]
        got = dict(zip(steps, lax.optimization_barrier(values)))
        got_x = [over_x[0]] + [got["x", k] for k in range(1, NX)]
        got_y = [over_y[0]] + [got["y", j] for j in range(1, NY)]
        return got_x, got_y

    with jax.named_scope("first_stage"):
        first, second = (sums(got) for got in exchange(by_x, by_y))

    with jax.named_scope("second_stage"):
        second_half, first_half = (total_of(got) for got in exchange(second, first))
        blocks = jnp.concatenate([first_half, second_half], axis=1).astype(jnp.bfloat16)

    with jax.named_scope("weights"):
        core = send(key_weight, "c", 1)
        held, blocks = lax.optimization_barrier((key_weight, blocks))
        other = cross(held)

    with jax.named_scope("third_stage"):
        parts = lax.all_to_all(blocks, "z", 0, 0, tiled=True)
        own_block = total_of([parts[n] for n in range(NZ)])

    with jax.named_scope("adam"):
        devices = NYL * NC * NZ * NYH * NX
        stored_grad = own_block * (tok_rows * devices) ** (-0.5)
        moment_one = beta_first * first_moment + (1.0 - beta_first) * stored_grad
        moment_two = beta_second * second_moment + (1.0 - beta_second) * stored_grad * stored_grad
        corrected_one = moment_one / (1.0 - beta_first**step_count)
        corrected_two = moment_two / (1.0 - beta_second**step_count)
        master_new = master_store - learn_rate * (
            corrected_one / (jnp.sqrt(corrected_two) + adam_eps) + decay_rate * master_store
        )

    with jax.named_scope("fresh_weights"):
        fresh = master_new.astype(jnp.bfloat16)
        most = width - width // 4

        def to_plane(value):
            value = jnp.broadcast_to(value, (NZ * NYH,) + value.shape)
            return lax.all_to_all(value, ("z", "yh"), 0, 0, tiled=True)

        plane = to_plane(fresh[:, :most])
        line = fresh[:, most:]
        line = jnp.stack([line] + [send(line, "x", k) for k in range(1, NX)])
        plane, line = lax.optimization_barrier((plane, line))
        parts = {k: send(plane, "x", k) for k in (1, 3, 2)}
        last_columns = to_plane(line)

    with jax.named_scope("input_grad"):
        place = jnp.stack([here + c, here + 1 - c]).astype(jnp.int32)
        input_grad = input_grad_of(place, key_cotangent, key_weight, core, depth)
        other, _ = lax.optimization_barrier((other, plane))
        other_core = send(other, "c", 1)
        place = jnp.stack([there + c, there + 1 - c]).astype(jnp.int32)
        input_grad = input_grad_of(place, key_cotangent, other, other_core, depth, input_grad)

    with jax.named_scope("rows"):
        near_x, near_back, input_grad = lax.optimization_barrier((parts[1], parts[3], input_grad))
        place = jnp.stack([x]).astype(jnp.int32)
        shape = key_weight.shape
        weight_new = None
        for group in ({0: plane, 1: near_x, 3: near_back}, {None: last_columns}, {2: parts[2]}):
            weight_new = put_in_rows(place, writer, group, shape, weight_new)
    return (input_grad, master_new, moment_one, moment_two, weight_new)


def solution(mesh):
    fine = Mesh(mesh.devices.reshape(NYL, NC, NZ, NYH, NX), AXES)
    shard, every = ("yl", "c"), AXES
    in_specs = (
        P(every, None),
        P(every, None),
        P(shard, None),
        P(every, None),
        P(every, None),
        P(every, None),
        P(shard, None),
    )
    out_specs = (P(every, None),) * 4 + (P(shard, None),)
    return jax.shard_map(
        on_device, mesh=fine, in_specs=in_specs, out_specs=out_specs, check_vma=False
    )
```

```python
import functools

import jax
import jax.numpy as jnp
from jax import lax
from jax.experimental import pallas as pl
from jax.experimental.pallas import tpu as pltpu
from jax.sharding import Mesh
from jax.sharding import PartitionSpec as P

beta_first = 0.9
beta_second = 0.95
learn_rate = 0.0003
decay_rate = 0.1
adam_eps = 1e-08
step_count = 100

NYL, NC, NZ, NYH, NX = 2, 2, 8, 2, 4
NY = NYL * NYH
AXES = ("yl", "c", "z", "yh", "x")
MIB = 1024 * 1024


def shift(axis, step):
    if axis == "y":
        spot = lambda y: (y % NYL) * NYH + y // NYL
        return [(spot(y), spot((y + step) % NY)) for y in range(NY)]
    size = {"x": NX, "z": NZ, "c": NC, "yl": NYL, "yh": NYH}[axis]
    return [(i, (i + step) % size) for i in range(size)]


def send(value, axis, step):
    return lax.ppermute(value, ("yl", "yh") if axis == "y" else axis, shift(axis, step))


def cross(value):
    pairs = []
    for y in range(NY):
        for c in range(NC):
            to = (y + 1 + 2 * c) % NY
            pairs.append(tuple(((n % NYL) * NC + c) * NYH + n // NYL for n in (y, to)))
    return lax.ppermute(value, ("yl", "c", "yh"), pairs)


def vmem():
    return pl.BlockSpec(memory_space=pltpu.VMEM)


def spec(block, index):
    return pl.BlockSpec(block, index)


def params(mib):
    return pltpu.CompilerParams(vmem_limit_bytes=mib * MIB)


def columns_kernel(place, tokens, far, near, sems):
    copies = []
    for n, out in enumerate((far, near)):
        rows = out.shape[1]
        start = pl.multiple_of(place[n] * rows, rows)
        copies.append(pltpu.make_async_copy(tokens.at[:, pl.ds(start, rows)], out, sems.at[n]))
    for copy in copies:
        copy.start()
    for copy in copies:
        copy.wait()


def columns_of(place, tokens, rows):
    shape = jax.ShapeDtypeStruct((tokens.shape[0], rows), tokens.dtype)
    return pl.pallas_call(
        columns_kernel,
        grid_spec=pltpu.PrefetchScalarGridSpec(
            num_scalar_prefetch=1,
            grid=(1,),
            in_specs=[pl.BlockSpec(memory_space=pl.ANY)],
            out_specs=[vmem(), vmem()],
            scratch_shapes=[pltpu.SemaphoreType.DMA((2,))],
        ),
        out_shape=[shape, shape],
        compiler_params=params(6),
    )(place, pltpu.with_memory_space_constraint(tokens, pltpu.HBM))


def partial_of(tok, key):
    value = lax.dot_general(tok, key, (((0,), (0,)), ((), ())), preferred_element_type=jnp.float32)
    return value.astype(jnp.bfloat16)


def own_kernel(place, tok, key, out):
    out[0] = partial_of(tok[...], key[...])


def own_partials(place, tokens, key, rows):
    cut = min(1024, rows)
    steps = rows // cut
    return pl.pallas_call(
        own_kernel,
        grid_spec=pltpu.PrefetchScalarGridSpec(
            num_scalar_prefetch=1,
            grid=(2, steps),
            in_specs=[
                spec((tokens.shape[0], cut), lambda n, q, place: (0, place[n] * steps + q)),
                spec(key.shape, lambda n, q, place: (0, 0)),
            ],
            out_specs=spec((1, cut, key.shape[1]), lambda n, q, place: (n, q, 0)),
        ),
        out_shape=jax.ShapeDtypeStruct((2, rows, key.shape[1]), jnp.bfloat16),
        compiler_params=params(8),
    )(place, pltpu.with_memory_space_constraint(tokens, pltpu.HBM), key)


def both_cores_kernel(place, far_order, near_order, own, far, near, key, *rest):
    by_x, by_y, total = rest[:NX], rest[NX : NX + NY], rest[-1]
    x, y = place[0], place[1]
    rows, half = total.shape[0], by_x[0].shape[2]
    cut = min(512, rows)
    for s, (tok, order) in enumerate(((far, far_order), (near, near_order))):
        for q in range(rows // cut):
            piece = slice(q * cut, (q + 1) * cut)
            got = partial_of(tok[:, piece], key[...])
            total[piece, :] = own[s, piece, :].astype(jnp.float32) + got.astype(jnp.float32)
        for j in (1 - s, 3 - s):
            to_yh = lax.div(lax.rem(y + j, NY), NYL)
            for k in range(NX):
                to_x = lax.rem(x + k, NX)
                for to_z in range(NZ):
                    block = order[0, (to_z * NYH + to_yh) * NX + to_x]
                    start = pl.multiple_of(block * (2 * half), 2 * half)
                    first = total[pl.ds(start, half), :]
                    second = total[pl.ds(start + half, half), :]
                    by_x[k][j, to_z] = first.astype(by_x[k].dtype)
                    by_y[j][k, to_z] = second.astype(by_y[j].dtype)


def both_cores(place, far_order, near_order, own, far, near, key, block_rows):
    rows, width = own.shape[1], own.shape[2]
    half = block_rows // 2
    shapes = [
        jax.ShapeDtypeStruct((count, NZ, half, width), jnp.bfloat16 if n else jnp.float32)
        for count, steps in ((NY, NX), (NX, NY))
        for n in range(steps)
    ]
    return pl.pallas_call(
        both_cores_kernel,
        grid_spec=pltpu.PrefetchScalarGridSpec(
            num_scalar_prefetch=3,
            grid=(1,),
            in_specs=[vmem()] * 4,
            out_specs=[vmem()] * len(shapes),
            scratch_shapes=[pltpu.VMEM((rows, width), jnp.float32)],
        ),
        out_shape=shapes,
        compiler_params=params(20),
    )(place, far_order, near_order, own, far, near, key)


def input_grad_kernel(count, place, key, *rest):
    out = rest[-1]
    for n, weight in enumerate(rest[:count]):

        @pl.when(lax.div(pl.program_id(0), 2) == n)
        def _(weight=weight):
            out[...] = lax.dot_general(
                key[...], weight[...], (((1,), (1,)), ((), ())), preferred_element_type=jnp.float32
            ).astype(out.dtype)


def input_grad_of(place, key, weights, width, before=None):
    count, cut = len(weights), weights[0].shape[0] // 2
    extra = [] if before is None else [before]

    def rows_of(n):
        return spec((cut, key.shape[1]), lambda i, place: (jnp.clip(i - 2 * n, 0, 1), 0))

    return pl.pallas_call(
        functools.partial(input_grad_kernel, count),
        grid_spec=pltpu.PrefetchScalarGridSpec(
            num_scalar_prefetch=1,
            grid=(2 * count,),
            in_specs=[spec(key.shape, lambda i, place: (0, 0))]
            + [rows_of(n) for n in range(count)]
            + [pl.BlockSpec(memory_space=pl.ANY)] * len(extra),
            out_specs=spec(
                (key.shape[0], cut),
                lambda i, place: (0, place[lax.div(i, 2)] * 2 + lax.rem(i, 2)),
            ),
        ),
        out_shape=jax.ShapeDtypeStruct((key.shape[0], width), jnp.bfloat16),
        input_output_aliases={2 + count: 0} if extra else {},
        compiler_params=params(12),
    )(place, key, *weights, *extra)


def rows_kernel(steps, place, order, *rest):
    parts, out, sems = rest[: len(steps)], rest[-2], rest[-1]
    x = place[0]
    block_rows = parts[0].shape[1]
    copies = []
    for part, (k, first) in zip(parts, steps):
        from_x = lax.rem(x + NX - k, NX)
        for n in range(part.shape[0]):
            block = order[0, (first + n) * NX + from_x]
            start = pl.multiple_of(block * block_rows, block_rows)
            copies.append(
                pltpu.make_async_copy(
                    part.at[n], out.at[pl.ds(start, block_rows), :], sems.at[len(copies)]
                )
            )
    for copy in copies:
        copy.start()
    for copy in copies:
        copy.wait()


def put_in_rows(place, order, parts, shape, before=None):
    steps, values = tuple(parts), list(parts.values())
    extra = [] if before is None else [before]
    return pl.pallas_call(
        functools.partial(rows_kernel, steps),
        grid_spec=pltpu.PrefetchScalarGridSpec(
            num_scalar_prefetch=2,
            grid=(1,),
            in_specs=[vmem()] * len(values) + [pl.BlockSpec(memory_space=pl.ANY)] * len(extra),
            out_specs=pl.BlockSpec(memory_space=pl.ANY),
            scratch_shapes=[pltpu.SemaphoreType.DMA((sum(v.shape[0] for v in values),))],
        ),
        out_shape=jax.ShapeDtypeStruct(shape, values[0].dtype),
        input_output_aliases={2 + len(values): 0} if extra else {},
        compiler_params=params(6),
    )(place, order, *values, *extra)


def f32(value):
    return value.astype(jnp.float32)


def total_of(values):
    total = f32(values[0])
    for value in values[1:]:
        total = total + f32(value)
    return total


def on_device(
    tokens_in, key_cotangent, key_weight, master_store, first_moment, second_moment, writer
):
    yl, c, _, yh, x = (lax.axis_index(name) for name in AXES)
    tok_rows, depth = tokens_in.shape
    width = key_weight.shape[1]
    rows_here = key_weight.shape[0]
    block_rows = master_store.shape[0]

    with jax.named_scope("core_swap"):
        here, there = yl * NC, (1 - yl) * NC
        got_key = send(key_cotangent, "c", 1)
        far_order = send(writer, "yl", 1)
        far, near = columns_of(
            jnp.stack([there + 1 - c, here + 1 - c]).astype(jnp.int32), tokens_in, rows_here
        )
        far, near = send(far, "c", 1), send(near, "c", 1)
        own = own_partials(
            jnp.stack([there + c, here + c]).astype(jnp.int32), tokens_in, key_cotangent, rows_here
        )
        place = jnp.stack([x, yh * NYL + yl]).astype(jnp.int32)
        parts = both_cores(place, far_order, writer, own, far, near, got_key, block_rows)
        by_x, by_y = list(parts[:NX]), list(parts[NX:])

    def sums(parts):
        values = [total_of([part[n] for part in parts]) for n in range(parts[0].shape[0])]
        return values[:1] + [value.astype(jnp.bfloat16) for value in values[1:]]

    def exchange(over_x, over_y):
        steps = [("x", 1), ("y", 1), ("y", 2), ("y", 3), ("x", 3), ("x", 2)]
        values = [send((over_x if axis == "x" else over_y)[n], axis, n) for axis, n in steps]
        got = dict(zip(steps, lax.optimization_barrier(values)))
        got_x = [over_x[0]] + [got["x", k] for k in range(1, NX)]
        got_y = [over_y[0]] + [got["y", j] for j in range(1, NY)]
        return got_x, got_y

    with jax.named_scope("first_stage"):
        first, second = (sums(got) for got in exchange(by_x, by_y))

    with jax.named_scope("second_stage"):
        second_half, first_half = (total_of(got) for got in exchange(second, first))
        blocks = jnp.concatenate([first_half, second_half], axis=1).astype(jnp.bfloat16)

    with jax.named_scope("weights"):
        core = send(key_weight, "c", 1)
        held, blocks = lax.optimization_barrier((key_weight, blocks))
        other = cross(held)

    with jax.named_scope("input_grad"):
        place = jnp.stack([here + c, here + 1 - c]).astype(jnp.int32)
        input_grad = input_grad_of(place, key_cotangent, [key_weight, core], depth)

    with jax.named_scope("third_stage"):
        parts = lax.all_to_all(blocks, "z", 0, 0, tiled=True)
        parts, input_grad = lax.optimization_barrier((parts, input_grad))
        own_block = total_of([parts[n] for n in range(NZ)])

    with jax.named_scope("adam"):
        devices = NYL * NC * NZ * NYH * NX
        stored_grad = own_block * (tok_rows * devices) ** (-0.5)
        moment_one = beta_first * first_moment + (1.0 - beta_first) * stored_grad
        moment_two = beta_second * second_moment + (1.0 - beta_second) * stored_grad * stored_grad
        corrected_one = moment_one / (1.0 - beta_first**step_count)
        corrected_two = moment_two / (1.0 - beta_second**step_count)
        master_new = master_store - learn_rate * (
            corrected_one / (jnp.sqrt(corrected_two) + adam_eps) + decay_rate * master_store
        )

    with jax.named_scope("fresh_weights"):
        fresh = master_new.astype(jnp.bfloat16)
        fresh = jnp.broadcast_to(fresh, (NZ * NYH,) + fresh.shape)
        plane = lax.all_to_all(fresh, ("z", "yh"), 0, 0, tiled=True)
        half = NZ * NYH // 2
        low, high = plane[:half], plane[half:]
        parts = {(1, 0): send(low, "x", 1), (3, half): send(high, "x", 3)}
        parts |= {(1, half): send(high, "x", 1), (3, 0): send(low, "x", 3)}
        last = {
            (2, 0): send(parts[1, 0], "x", 1),
            (2, half): send(parts[3, half], "x", 3),
        }

    with jax.named_scope("input_grad"):
        other, _ = lax.optimization_barrier((other, plane))
        other_core = send(other, "c", 1)
        place = jnp.stack([there + c, there + 1 - c]).astype(jnp.int32)
        input_grad = input_grad_of(
            place, key_cotangent, [other, other_core], depth, input_grad
        )

    with jax.named_scope("rows"):
        *values, input_grad = lax.optimization_barrier((*parts.values(), input_grad))
        parts = {(0, 0): plane} | dict(zip(parts, values))
        place = jnp.stack([x]).astype(jnp.int32)
        weight_new = put_in_rows(place, writer, parts, key_weight.shape)
        weight_new = put_in_rows(place, writer, last, key_weight.shape, weight_new)
    return (input_grad, master_new, moment_one, moment_two, weight_new)


def solution(mesh):
    fine = Mesh(mesh.devices.reshape(NYL, NC, NZ, NYH, NX), AXES)
    shard, every = ("yl", "c"), AXES
    in_specs = (
        P(every, None),
        P(every, None),
        P(shard, None),
        P(every, None),
        P(every, None),
        P(every, None),
        P(shard, None),
    )
    out_specs = (P(every, None),) * 4 + (P(shard, None),)
    return jax.shard_map(
        on_device, mesh=fine, in_specs=in_specs, out_specs=out_specs, check_vma=False
    )
```

```python
import functools

import jax
import jax.numpy as jnp
from jax import lax
from jax.experimental import pallas as pl
from jax.experimental.pallas import tpu as pltpu
from jax.sharding import Mesh
from jax.sharding import PartitionSpec as P

beta_first = 0.9
beta_second = 0.95
learn_rate = 0.0003
decay_rate = 0.1
adam_eps = 1e-08
step_count = 100

NYL, NC, NZ, NYH, NX = 2, 2, 8, 2, 4
NY = NYL * NYH
AXES = ("yl", "c", "z", "yh", "x")
MIB = 1024 * 1024


def shift(axis, step):
    if axis == "y":
        spot = lambda y: (y % NYL) * NYH + y // NYL
        return [(spot(y), spot((y + step) % NY)) for y in range(NY)]
    size = {"x": NX, "z": NZ, "c": NC, "yl": NYL, "yh": NYH}[axis]
    return [(i, (i + step) % size) for i in range(size)]


def send(value, axis, step):
    return lax.ppermute(value, ("yl", "yh") if axis == "y" else axis, shift(axis, step))


def cross(value):
    pairs = []
    for y in range(NY):
        for c in range(NC):
            to = (y + 1 + 2 * c) % NY
            pairs.append(tuple(((n % NYL) * NC + c) * NYH + n // NYL for n in (y, to)))
    return lax.ppermute(value, ("yl", "c", "yh"), pairs)


def vmem():
    return pl.BlockSpec(memory_space=pltpu.VMEM)


def spec(block, index):
    return pl.BlockSpec(block, index)


def params(mib):
    return pltpu.CompilerParams(vmem_limit_bytes=mib * MIB)


def columns_kernel(place, tokens, far, near, held, sems):
    rows, pieces = held.shape[2], sems.shape[2]
    cut = held.shape[1] // pieces
    inward, outward = [], []
    for n, out in enumerate((far, near)):
        start = pl.multiple_of(place[n] * rows, rows)
        for i in range(pieces):
            here = pl.ds(i * cut, cut)
            inward.append(
                pltpu.make_async_copy(
                    tokens.at[here, pl.ds(start, rows)], held.at[n, here, :], sems.at[0, n, i]
                )
            )
            outward.append(
                pltpu.make_async_copy(held.at[n, here, :], out.at[here, :], sems.at[1, n, i])
            )
    for copy in inward:
        copy.start()
    for copy, after in zip(inward, outward):
        copy.wait()
        after.start()
    for copy in outward:
        copy.wait()


def columns_of(place, tokens, rows):
    count = tokens.shape[0]
    pieces = 4 if count % 64 == 0 else 1
    shape = jax.ShapeDtypeStruct((count, rows), tokens.dtype)
    return pl.pallas_call(
        columns_kernel,
        grid_spec=pltpu.PrefetchScalarGridSpec(
            num_scalar_prefetch=1,
            grid=(1,),
            in_specs=[pl.BlockSpec(memory_space=pl.ANY)],
            out_specs=[pl.BlockSpec(memory_space=pl.ANY)] * 2,
            scratch_shapes=[
                pltpu.VMEM((2, count, rows), tokens.dtype),
                pltpu.SemaphoreType.DMA((2, 2, pieces)),
            ],
        ),
        out_shape=[shape, shape],
        compiler_params=params(6),
    )(place, pltpu.with_memory_space_constraint(tokens, pltpu.HBM))


def partial_of(tok, key):
    value = lax.dot_general(tok, key, (((0,), (0,)), ((), ())), preferred_element_type=jnp.float32)
    return value.astype(jnp.bfloat16)


def own_kernel(place, tok, key, out):
    out[0] = partial_of(tok[...], key[...])


def own_partials(place, tokens, key, rows):
    cut = min(1024, rows)
    steps = rows // cut
    return pl.pallas_call(
        own_kernel,
        grid_spec=pltpu.PrefetchScalarGridSpec(
            num_scalar_prefetch=1,
            grid=(2, steps),
            in_specs=[
                spec((tokens.shape[0], cut), lambda n, q, place: (0, place[n] * steps + q)),
                spec(key.shape, lambda n, q, place: (0, 0)),
            ],
            out_specs=spec((1, cut, key.shape[1]), lambda n, q, place: (n, q, 0)),
        ),
        out_shape=jax.ShapeDtypeStruct((2, rows, key.shape[1]), jnp.bfloat16),
        compiler_params=params(8),
    )(place, pltpu.with_memory_space_constraint(tokens, pltpu.HBM), key)


def both_cores_kernel(place, far_order, near_order, own, far, near, key, *rest):
    by_x, by_y, total = rest[:NX], rest[NX : NX + NY], rest[-1]
    x, y = place[0], place[1]
    rows, half = total.shape[0], by_x[0].shape[2]
    cut = min(512, rows)
    for s, (tok, order) in enumerate(((far, far_order), (near, near_order))):
        for q in range(rows // cut):
            piece = slice(q * cut, (q + 1) * cut)
            got = partial_of(tok[:, piece], key[...])
            total[piece, :] = own[s, piece, :].astype(jnp.float32) + got.astype(jnp.float32)
        for j in (1 - s, 3 - s):
            to_yh = lax.div(lax.rem(y + j, NY), NYL)
            for k in range(NX):
                to_x = lax.rem(x + k, NX)
                for to_z in range(NZ):
                    block = order[0, (to_z * NYH + to_yh) * NX + to_x]
                    start = pl.multiple_of(block * (2 * half), 2 * half)
                    first = total[pl.ds(start, half), :]
                    second = total[pl.ds(start + half, half), :]
                    by_x[k][j, to_z] = first.astype(by_x[k].dtype)
                    by_y[j][k, to_z] = second.astype(by_y[j].dtype)


def both_cores(place, far_order, near_order, own, far, near, key, block_rows):
    rows, width = own.shape[1], own.shape[2]
    half = block_rows // 2
    shapes = [
        jax.ShapeDtypeStruct((count, NZ, half, width), jnp.bfloat16 if n else jnp.float32)
        for count, steps in ((NY, NX), (NX, NY))
        for n in range(steps)
    ]
    return pl.pallas_call(
        both_cores_kernel,
        grid_spec=pltpu.PrefetchScalarGridSpec(
            num_scalar_prefetch=3,
            grid=(1,),
            in_specs=[vmem()] * 4,
            out_specs=[vmem()] * len(shapes),
            scratch_shapes=[pltpu.VMEM((rows, width), jnp.float32)],
        ),
        out_shape=shapes,
        compiler_params=params(20),
    )(place, far_order, near_order, own, far, near, key)


def input_grad_kernel(count, place, key, *rest):
    out = rest[-1]
    for n, weight in enumerate(rest[:count]):

        @pl.when(lax.div(pl.program_id(0), 2) == n)
        def _(weight=weight):
            out[...] = lax.dot_general(
                key[...], weight[...], (((1,), (1,)), ((), ())), preferred_element_type=jnp.float32
            ).astype(out.dtype)


def input_grad_of(place, key, weights, width, before=None):
    count, cut = len(weights), weights[0].shape[0] // 2
    extra = [] if before is None else [before]

    def rows_of(n):
        return spec((cut, key.shape[1]), lambda i, place: (jnp.clip(i - 2 * n, 0, 1), 0))

    return pl.pallas_call(
        functools.partial(input_grad_kernel, count),
        grid_spec=pltpu.PrefetchScalarGridSpec(
            num_scalar_prefetch=1,
            grid=(2 * count,),
            in_specs=[spec(key.shape, lambda i, place: (0, 0))]
            + [rows_of(n) for n in range(count)]
            + [pl.BlockSpec(memory_space=pl.ANY)] * len(extra),
            out_specs=spec(
                (key.shape[0], cut),
                lambda i, place: (0, place[lax.div(i, 2)] * 2 + lax.rem(i, 2)),
            ),
        ),
        out_shape=jax.ShapeDtypeStruct((key.shape[0], width), jnp.bfloat16),
        input_output_aliases={2 + count: 0} if extra else {},
        compiler_params=params(12),
    )(place, key, *weights, *extra)


def rows_kernel(steps, place, order, *rest):
    parts, out, sems = rest[: len(steps)], rest[-2], rest[-1]
    x = place[0]
    block_rows = parts[0].shape[1]
    copies = []
    for part, (k, first) in zip(parts, steps):
        from_x = lax.rem(x + NX - k, NX)
        for n in range(part.shape[0]):
            block = order[0, (first + n) * NX + from_x]
            start = pl.multiple_of(block * block_rows, block_rows)
            copies.append(
                pltpu.make_async_copy(
                    part.at[n], out.at[pl.ds(start, block_rows), :], sems.at[len(copies)]
                )
            )
    for copy in copies:
        copy.start()
    for copy in copies:
        copy.wait()


def put_in_rows(place, order, parts, shape, before=None):
    steps, values = tuple(parts), list(parts.values())
    extra = [] if before is None else [before]
    return pl.pallas_call(
        functools.partial(rows_kernel, steps),
        grid_spec=pltpu.PrefetchScalarGridSpec(
            num_scalar_prefetch=2,
            grid=(1,),
            in_specs=[vmem()] * len(values) + [pl.BlockSpec(memory_space=pl.ANY)] * len(extra),
            out_specs=pl.BlockSpec(memory_space=pl.ANY),
            scratch_shapes=[pltpu.SemaphoreType.DMA((sum(v.shape[0] for v in values),))],
        ),
        out_shape=jax.ShapeDtypeStruct(shape, values[0].dtype),
        input_output_aliases={2 + len(values): 0} if extra else {},
        compiler_params=params(6),
    )(place, order, *values, *extra)


def f32(value):
    return value.astype(jnp.float32)


def total_of(values):
    total = f32(values[0])
    for value in values[1:]:
        total = total + f32(value)
    return total


def on_device(
    tokens_in, key_cotangent, key_weight, master_store, first_moment, second_moment, writer
):
    yl, c, _, yh, x = (lax.axis_index(name) for name in AXES)
    tok_rows, depth = tokens_in.shape
    width = key_weight.shape[1]
    rows_here = key_weight.shape[0]
    block_rows = master_store.shape[0]

    with jax.named_scope("core_swap"):
        here, there = yl * NC, (1 - yl) * NC
        got_key = send(key_cotangent, "c", 1)
        far_order = send(writer, "yl", 1)
        far, near = columns_of(
            jnp.stack([there + 1 - c, here + 1 - c]).astype(jnp.int32), tokens_in, rows_here
        )
        far, near = send(far, "c", 1), send(near, "c", 1)
        own = own_partials(
            jnp.stack([there + c, here + c]).astype(jnp.int32), tokens_in, key_cotangent, rows_here
        )
        place = jnp.stack([x, yh * NYL + yl]).astype(jnp.int32)
        parts = both_cores(place, far_order, writer, own, far, near, got_key, block_rows)
        by_x, by_y = list(parts[:NX]), list(parts[NX:])

    def sums(parts):
        values = [total_of([part[n] for part in parts]) for n in range(parts[0].shape[0])]
        return values[:1] + [value.astype(jnp.bfloat16) for value in values[1:]]

    def exchange(over_x, over_y):
        steps = [("x", 1), ("y", 1), ("y", 2), ("y", 3), ("x", 3), ("x", 2)]
        values = [send((over_x if axis == "x" else over_y)[n], axis, n) for axis, n in steps]
        got = dict(zip(steps, lax.optimization_barrier(values)))
        got_x = [over_x[0]] + [got["x", k] for k in range(1, NX)]
        got_y = [over_y[0]] + [got["y", j] for j in range(1, NY)]
        return got_x, got_y

    with jax.named_scope("first_stage"):
        first, second = (sums(got) for got in exchange(by_x, by_y))

    with jax.named_scope("second_stage"):
        second_half, first_half = (total_of(got) for got in exchange(second, first))
        blocks = jnp.concatenate([first_half, second_half], axis=1).astype(jnp.bfloat16)

    with jax.named_scope("weights"):
        held, blocks = lax.optimization_barrier((key_weight, blocks))
        core = send(held, "c", 1)
        other = cross(held)
        place = jnp.stack([here + c, here + 1 - c]).astype(jnp.int32)
        input_grad = input_grad_of(place, key_cotangent, [held, core], depth)

    with jax.named_scope("third_stage"):
        parts = lax.all_to_all(blocks, "z", 0, 0, tiled=True)
        parts, input_grad = lax.optimization_barrier((parts, input_grad))
        own_block = total_of([parts[n] for n in range(NZ)])

    with jax.named_scope("adam"):
        devices = NYL * NC * NZ * NYH * NX
        stored_grad = own_block * (tok_rows * devices) ** (-0.5)
        moment_one = beta_first * first_moment + (1.0 - beta_first) * stored_grad
        moment_two = beta_second * second_moment + (1.0 - beta_second) * stored_grad * stored_grad
        corrected_one = moment_one / (1.0 - beta_first**step_count)
        corrected_two = moment_two / (1.0 - beta_second**step_count)
        master_new = master_store - learn_rate * (
            corrected_one / (jnp.sqrt(corrected_two) + adam_eps) + decay_rate * master_store
        )

    with jax.named_scope("fresh_weights"):
        fresh = master_new.astype(jnp.bfloat16)
        fresh = jnp.broadcast_to(fresh, (NZ * NYH,) + fresh.shape)
        plane = lax.all_to_all(fresh, ("z", "yh"), 0, 0, tiled=True)
        half = NZ * NYH // 2
        low, high = plane[:half], plane[half:]
        parts = {(1, 0): send(low, "x", 1), (3, half): send(high, "x", 3)}
        parts |= {(1, half): send(high, "x", 1), (3, 0): send(low, "x", 3)}
        last = {
            (2, 0): send(parts[1, 0], "x", 1),
            (2, half): send(parts[3, half], "x", 3),
        }

    with jax.named_scope("input_grad"):
        other, _ = lax.optimization_barrier((other, plane))
        other_core = send(other, "c", 1)
        place = jnp.stack([there + c, there + 1 - c]).astype(jnp.int32)
        input_grad = input_grad_of(
            place, key_cotangent, [other, other_core], depth, input_grad
        )

    with jax.named_scope("rows"):
        *values, input_grad = lax.optimization_barrier((*parts.values(), input_grad))
        parts = {(0, 0): plane} | dict(zip(parts, values))
        place = jnp.stack([x]).astype(jnp.int32)
        weight_new = put_in_rows(place, writer, parts, key_weight.shape)
        weight_new = put_in_rows(place, writer, last, key_weight.shape, weight_new)
    return (input_grad, master_new, moment_one, moment_two, weight_new)


def solution(mesh):
    fine = Mesh(mesh.devices.reshape(NYL, NC, NZ, NYH, NX), AXES)
    shard, every = ("yl", "c"), AXES
    in_specs = (
        P(every, None),
        P(every, None),
        P(shard, None),
        P(every, None),
        P(every, None),
        P(every, None),
        P(shard, None),
    )
    out_specs = (P(every, None),) * 4 + (P(shard, None),)
    return jax.shard_map(
        on_device, mesh=fine, in_specs=in_specs, out_specs=out_specs, check_vma=False
    )
```

```python
import functools

import jax
import jax.numpy as jnp
from jax import lax
from jax.experimental import pallas as pl
from jax.experimental.pallas import tpu as pltpu
from jax.sharding import Mesh
from jax.sharding import PartitionSpec as P

beta_first = 0.9
beta_second = 0.95
learn_rate = 0.0003
decay_rate = 0.1
adam_eps = 1e-08
step_count = 100

NYL, NC, NZ, NYH, NX = 2, 2, 8, 2, 4
NY = NYL * NYH
AXES = ("yl", "c", "z", "yh", "x")
MIB = 1024 * 1024


def shift(axis, step):
    if axis == "y":
        spot = lambda y: (y % NYL) * NYH + y // NYL
        return [(spot(y), spot((y + step) % NY)) for y in range(NY)]
    size = {"x": NX, "z": NZ, "c": NC, "yl": NYL, "yh": NYH}[axis]
    return [(i, (i + step) % size) for i in range(size)]


def send(value, axis, step):
    return lax.ppermute(value, ("yl", "yh") if axis == "y" else axis, shift(axis, step))


def cross(value):
    pairs = []
    for y in range(NY):
        for c in range(NC):
            to = (y + 1 + 2 * c) % NY
            pairs.append(tuple(((n % NYL) * NC + c) * NYH + n // NYL for n in (y, to)))
    return lax.ppermute(value, ("yl", "c", "yh"), pairs)


def vmem():
    return pl.BlockSpec(memory_space=pltpu.VMEM)


def spec(block, index):
    return pl.BlockSpec(block, index)


def params(mib):
    return pltpu.CompilerParams(vmem_limit_bytes=mib * MIB)


def columns_kernel(place, tokens, far, near, held, sems):
    rows, pieces = held.shape[2], sems.shape[2]
    cut = held.shape[1] // pieces
    inward, outward = [], []
    for n, out in enumerate((far, near)):
        start = pl.multiple_of(place[n] * rows, rows)
        for i in range(pieces):
            here = pl.ds(i * cut, cut)
            inward.append(
                pltpu.make_async_copy(
                    tokens.at[here, pl.ds(start, rows)], held.at[n, here, :], sems.at[0, n, i]
                )
            )
            outward.append(
                pltpu.make_async_copy(held.at[n, here, :], out.at[here, :], sems.at[1, n, i])
            )
    for copy in inward:
        copy.start()
    for copy, after in zip(inward, outward):
        copy.wait()
        after.start()
    for copy in outward:
        copy.wait()


def columns_of(place, tokens, rows):
    count = tokens.shape[0]
    pieces = 4 if count % 64 == 0 else 1
    shape = jax.ShapeDtypeStruct((count, rows), tokens.dtype)
    return pl.pallas_call(
        columns_kernel,
        grid_spec=pltpu.PrefetchScalarGridSpec(
            num_scalar_prefetch=1,
            grid=(1,),
            in_specs=[pl.BlockSpec(memory_space=pl.ANY)],
            out_specs=[pl.BlockSpec(memory_space=pl.ANY)] * 2,
            scratch_shapes=[
                pltpu.VMEM((2, count, rows), tokens.dtype),
                pltpu.SemaphoreType.DMA((2, 2, pieces)),
            ],
        ),
        out_shape=[shape, shape],
        compiler_params=params(6),
    )(place, pltpu.with_memory_space_constraint(tokens, pltpu.HBM))


def partial_of(tok, key):
    value = lax.dot_general(tok, key, (((0,), (0,)), ((), ())), preferred_element_type=jnp.float32)
    return value.astype(jnp.bfloat16)


def own_kernel(place, tok, key, out):
    out[0] = partial_of(tok[...], key[...])


def own_partials(place, tokens, key, rows):
    cut = min(1024, rows)
    steps = rows // cut
    return pl.pallas_call(
        own_kernel,
        grid_spec=pltpu.PrefetchScalarGridSpec(
            num_scalar_prefetch=1,
            grid=(2, steps),
            in_specs=[
                spec((tokens.shape[0], cut), lambda n, q, place: (0, place[n] * steps + q)),
                spec(key.shape, lambda n, q, place: (0, 0)),
            ],
            out_specs=spec((1, cut, key.shape[1]), lambda n, q, place: (n, q, 0)),
        ),
        out_shape=jax.ShapeDtypeStruct((2, rows, key.shape[1]), jnp.bfloat16),
        compiler_params=params(8),
    )(place, pltpu.with_memory_space_constraint(tokens, pltpu.HBM), key)


def both_cores_kernel(place, far_order, near_order, own, far, near, key, *rest):
    by_x, by_y, total = rest[:NX], rest[NX : NX + NY], rest[-1]
    x, y = place[0], place[1]
    rows, half = total.shape[0], by_x[0].shape[2]
    cut = min(512, rows)
    for s, (tok, order) in enumerate(((far, far_order), (near, near_order))):
        for q in range(rows // cut):
            piece = slice(q * cut, (q + 1) * cut)
            got = partial_of(tok[:, piece], key[...])
            total[piece, :] = own[s, piece, :].astype(jnp.float32) + got.astype(jnp.float32)
        for j in (1 - s, 3 - s):
            to_yh = lax.div(lax.rem(y + j, NY), NYL)
            for k in range(NX):
                to_x = lax.rem(x + k, NX)
                for to_z in range(NZ):
                    block = order[0, (to_z * NYH + to_yh) * NX + to_x]
                    start = pl.multiple_of(block * (2 * half), 2 * half)
                    first = total[pl.ds(start, half), :]
                    second = total[pl.ds(start + half, half), :]
                    by_x[k][j, to_z] = first.astype(by_x[k].dtype)
                    by_y[j][k, to_z] = second.astype(by_y[j].dtype)


def both_cores(place, far_order, near_order, own, far, near, key, block_rows):
    rows, width = own.shape[1], own.shape[2]
    half = block_rows // 2
    shapes = [
        jax.ShapeDtypeStruct((count, NZ, half, width), jnp.bfloat16 if n else jnp.float32)
        for count, steps in ((NY, NX), (NX, NY))
        for n in range(steps)
    ]
    return pl.pallas_call(
        both_cores_kernel,
        grid_spec=pltpu.PrefetchScalarGridSpec(
            num_scalar_prefetch=3,
            grid=(1,),
            in_specs=[vmem()] * 4,
            out_specs=[vmem()] * len(shapes),
            scratch_shapes=[pltpu.VMEM((rows, width), jnp.float32)],
        ),
        out_shape=shapes,
        compiler_params=params(20),
    )(place, far_order, near_order, own, far, near, key)


def input_grad_kernel(count, place, key, *rest):
    out = rest[-1]
    for n, weight in enumerate(rest[:count]):

        @pl.when(lax.div(pl.program_id(0), 2) == n)
        def _(weight=weight):
            out[...] = lax.dot_general(
                key[...], weight[...], (((1,), (1,)), ((), ())), preferred_element_type=jnp.float32
            ).astype(out.dtype)


def input_grad_of(place, key, weights, width, before=None):
    count, cut = len(weights), weights[0].shape[0] // 2
    extra = [] if before is None else [before]

    def rows_of(n):
        return spec((cut, key.shape[1]), lambda i, place: (jnp.clip(i - 2 * n, 0, 1), 0))

    return pl.pallas_call(
        functools.partial(input_grad_kernel, count),
        grid_spec=pltpu.PrefetchScalarGridSpec(
            num_scalar_prefetch=1,
            grid=(2 * count,),
            in_specs=[spec(key.shape, lambda i, place: (0, 0))]
            + [rows_of(n) for n in range(count)]
            + [pl.BlockSpec(memory_space=pl.ANY)] * len(extra),
            out_specs=spec(
                (key.shape[0], cut),
                lambda i, place: (0, place[lax.div(i, 2)] * 2 + lax.rem(i, 2)),
            ),
        ),
        out_shape=jax.ShapeDtypeStruct((key.shape[0], width), jnp.bfloat16),
        input_output_aliases={2 + count: 0} if extra else {},
        compiler_params=params(12),
    )(place, key, *weights, *extra)


def rows_kernel(steps, place, order, *rest):
    parts, out, sems = rest[: len(steps)], rest[-2], rest[-1]
    x = place[0]
    block_rows = parts[0].shape[1]
    copies = []
    for part, (k, first) in zip(parts, steps):
        from_x = lax.rem(x + NX - k, NX)
        for n in range(part.shape[0]):
            block = order[0, (first + n) * NX + from_x]
            start = pl.multiple_of(block * block_rows, block_rows)
            copies.append(
                pltpu.make_async_copy(
                    part.at[n], out.at[pl.ds(start, block_rows), :], sems.at[len(copies)]
                )
            )
    for copy in copies:
        copy.start()
    for copy in copies:
        copy.wait()


def put_in_rows(place, order, parts, shape, before=None):
    steps, values = tuple(parts), list(parts.values())
    extra = [] if before is None else [before]
    return pl.pallas_call(
        functools.partial(rows_kernel, steps),
        grid_spec=pltpu.PrefetchScalarGridSpec(
            num_scalar_prefetch=2,
            grid=(1,),
            in_specs=[vmem()] * len(values) + [pl.BlockSpec(memory_space=pl.ANY)] * len(extra),
            out_specs=pl.BlockSpec(memory_space=pl.ANY),
            scratch_shapes=[pltpu.SemaphoreType.DMA((sum(v.shape[0] for v in values),))],
        ),
        out_shape=jax.ShapeDtypeStruct(shape, values[0].dtype),
        input_output_aliases={2 + len(values): 0} if extra else {},
        compiler_params=params(6),
    )(place, order, *values, *extra)


def f32(value):
    return value.astype(jnp.float32)


def total_of(values):
    total = f32(values[0])
    for value in values[1:]:
        total = total + f32(value)
    return total


def on_device(
    tokens_in, key_cotangent, key_weight, master_store, first_moment, second_moment, writer
):
    yl, c, _, yh, x = (lax.axis_index(name) for name in AXES)
    tok_rows, depth = tokens_in.shape
    width = key_weight.shape[1]
    rows_here = key_weight.shape[0]
    block_rows = master_store.shape[0]

    with jax.named_scope("core_swap"):
        here, there = yl * NC, (1 - yl) * NC
        got_key = send(key_cotangent, "c", 1)
        far_order = send(writer, "yl", 1)
        far, near = columns_of(
            jnp.stack([there + 1 - c, here + 1 - c]).astype(jnp.int32), tokens_in, rows_here
        )
        far, near = send(far, "c", 1), send(near, "c", 1)
        own = own_partials(
            jnp.stack([there + c, here + c]).astype(jnp.int32), tokens_in, key_cotangent, rows_here
        )
        place = jnp.stack([x, yh * NYL + yl]).astype(jnp.int32)
        parts = both_cores(place, far_order, writer, own, far, near, got_key, block_rows)
        by_x, by_y = list(parts[:NX]), list(parts[NX:])

    def sums(parts):
        values = [total_of([part[n] for part in parts]) for n in range(parts[0].shape[0])]
        return values[:1] + [value.astype(jnp.bfloat16) for value in values[1:]]

    def exchange(over_x, over_y):
        steps = [("x", 1), ("y", 1), ("y", 2), ("y", 3), ("x", 3), ("x", 2)]
        values = [send((over_x if axis == "x" else over_y)[n], axis, n) for axis, n in steps]
        got = dict(zip(steps, lax.optimization_barrier(values)))
        got_x = [over_x[0]] + [got["x", k] for k in range(1, NX)]
        got_y = [over_y[0]] + [got["y", j] for j in range(1, NY)]
        return got_x, got_y

    with jax.named_scope("first_stage"):
        first, second = (sums(got) for got in exchange(by_x, by_y))

    with jax.named_scope("second_stage"):
        second_half, first_half = (total_of(got) for got in exchange(second, first))
        blocks = jnp.concatenate([first_half, second_half], axis=1).astype(jnp.bfloat16)

    with jax.named_scope("weights"):
        held, blocks = lax.optimization_barrier((key_weight, blocks))
        other = cross(held)

    with jax.named_scope("input_grad"):
        place = jnp.stack([here + c]).astype(jnp.int32)
        input_grad = input_grad_of(place, key_cotangent, [key_weight], depth)

    with jax.named_scope("third_stage"):
        parts = lax.all_to_all(blocks, "z", 0, 0, tiled=True)
        parts, input_grad = lax.optimization_barrier((parts, input_grad))
        held, parts = lax.optimization_barrier((key_weight, parts))
        core = send(held, "c", 1)
        own_block = total_of([parts[n] for n in range(NZ)])

    with jax.named_scope("adam"):
        devices = NYL * NC * NZ * NYH * NX
        stored_grad = own_block * (tok_rows * devices) ** (-0.5)
        moment_one = beta_first * first_moment + (1.0 - beta_first) * stored_grad
        moment_two = beta_second * second_moment + (1.0 - beta_second) * stored_grad * stored_grad
        corrected_one = moment_one / (1.0 - beta_first**step_count)
        corrected_two = moment_two / (1.0 - beta_second**step_count)
        master_new = master_store - learn_rate * (
            corrected_one / (jnp.sqrt(corrected_two) + adam_eps) + decay_rate * master_store
        )

    with jax.named_scope("fresh_weights"):
        fresh = master_new.astype(jnp.bfloat16)
        fresh = jnp.broadcast_to(fresh, (NZ * NYH,) + fresh.shape)
        plane = lax.all_to_all(fresh, ("z", "yh"), 0, 0, tiled=True)
        plane, core = lax.optimization_barrier((plane, core))
        half = NZ * NYH // 2
        low, high = plane[:half], plane[half:]
        parts = {(1, 0): send(low, "x", 1), (3, half): send(high, "x", 3)}
        parts |= {(1, half): send(high, "x", 1), (3, 0): send(low, "x", 3)}
        last = {
            (2, 0): send(parts[1, 0], "x", 1),
            (2, half): send(parts[3, half], "x", 3),
        }

    with jax.named_scope("input_grad"):
        other, _ = lax.optimization_barrier((other, plane))
        other_core = send(other, "c", 1)
        place = jnp.stack([here + 1 - c, there + c, there + 1 - c]).astype(jnp.int32)
        input_grad = input_grad_of(
            place, key_cotangent, [core, other, other_core], depth, input_grad
        )

    with jax.named_scope("rows"):
        *values, input_grad = lax.optimization_barrier((*parts.values(), input_grad))
        parts = {(0, 0): plane} | dict(zip(parts, values))
        place = jnp.stack([x]).astype(jnp.int32)
        weight_new = put_in_rows(place, writer, parts, key_weight.shape)
        weight_new = put_in_rows(place, writer, last, key_weight.shape, weight_new)
    return (input_grad, master_new, moment_one, moment_two, weight_new)


def solution(mesh):
    fine = Mesh(mesh.devices.reshape(NYL, NC, NZ, NYH, NX), AXES)
    shard, every = ("yl", "c"), AXES
    in_specs = (
        P(every, None),
        P(every, None),
        P(shard, None),
        P(every, None),
        P(every, None),
        P(every, None),
        P(shard, None),
    )
    out_specs = (P(every, None),) * 4 + (P(shard, None),)
    return jax.shard_map(
        on_device, mesh=fine, in_specs=in_specs, out_specs=out_specs, check_vma=False
    )
```
